256 devices in a mesh: section: 16 (over y, z_hi), tp: 16 (over x, z_lo, core).
Axes of the slice: x: 4, y: 4, z: 8 (z_hi: 4, z_lo: 2; z = z_hi * 2 + z_lo), core: 2. Of those that a mesh axis runs over, the one named last changes fastest.
Arguments:
- image_rows: bfloat16 [384, 8192], P('section', 'tp'), may hold values from -6 to 6
- queries: bfloat16 [16, 512, 8192], P('section', None, 'tp'), may hold values from -6 to 6
- key_weight: bfloat16 [16, 8192, 1024], P('section', 'tp'), may hold values from -0.0625 to 0.0625
- value_weight: bfloat16 [16, 8192, 1024], P('section', 'tp'), may hold values from -0.0625 to 0.0625
- query_gain: float32 [16, 128], P('section'), may hold values from 0.5 to 2
- key_gain: float32 [16, 128], P('section'), may hold values from 0.5 to 2
- tiles_seen: int32 [512], replicated, may hold values from 0 to 4
- context_grad: bfloat16 [16, 512, 8192], P('section', None, 'tp'), may hold values from -6 to 6
Outputs:
- context: bfloat16 [16, 512, 8192], P('section', None, 'tp')
- query_grad: bfloat16 [16, 512, 8192], P('section', None, 'tp')
- key_weight_grad: bfloat16 [16, 8192, 1024], P('section', 'tp')
- value_weight_grad: bfloat16 [16, 8192, 1024], P('section', 'tp')
- image_grad: float32 [384, 8192], P('section', 'tp')
The draws below stay inside these ranges and needn't reach their ends.
Inputs may be any that keep to these rules, and one draw needn't show every extreme that they name: `tiles_seen`: tiles are counted from the image's first; 0 means the row attends no image row and its attention output is zero.
All inputs are finite; a program needn't handle non-finite values.
Results may differ from the reference program's by a relative error of at most 0.019.
Values may be sent and summed in bfloat16 or wider, within the bound.
No kernel may reach another device: no remote copies, remote signals or barrier semaphores. Data moves between devices by JAX's collectives and lax.ppermute only.
A program may use at most 64 MiB of HBM per device.

```python
import jax
import jax.numpy as jnp
from jax import lax

D = 8192
KVH = 8
HD = 128
TEXT = 512
TILE_ROWS = 96
TILES = 4
IMG = 384
QD = 8192
KVD = 1024
GROUP = 8
N_SECTION = 16


def with_ends(entries, rng, least, largest):
    longest = entries.shape.index(max(entries.shape))
    spots = []
    for shift in (0, 1):
        where = [jax.random.randint(jax.random.fold_in(rng, axis), (), 0, length) for axis, length in enumerate(entries.shape)]
        where[longest] = (where[longest] + shift) % entries.shape[longest]
        spots.append(tuple(where))
    return entries.at[spots[0]].set(least).at[spots[1]].set(largest)


def block_scale(key, shape, cuts, least, top_value):
    def one(dim, shards_of):
        heights = jax.random.uniform(jax.random.fold_in(jax.random.fold_in(key, 6), dim), (shards_of,), jnp.float32, least / len(cuts), top_value / len(cuts))
        return jnp.repeat(jnp.exp(heights), shape[dim] // shards_of).reshape((-1,) + (1,) * (len(shape) - dim - 1))

    gain = one(*cuts[0])
    for cut in cuts[1:]:
        gain = gain * one(*cut)
    return gain


def normal_values(key, dims, scale, most, cuts=(), kind=jnp.bfloat16):
    array = jax.random.normal(key, dims, jnp.float32) * scale
    if len(cuts) > 0:
        array = block_scale(key, dims, cuts, -0.22, 0.18) * array
    return jnp.clip(array, min=-most, max=most).astype(kind)


def setup_inputs(seed: int = 0) -> dict:
    splits = jax.random.split(jax.random.key(seed), 9)
    return {
        "image_rows": normal_values(splits[0], (IMG, D), 1.0, 6.0, ((0, 16), (1, 16))),
        "queries": normal_values(splits[1], (N_SECTION, TEXT, QD), 1.0, 6.0, ((0, 16), (2, 16))),
        "key_weight": normal_values(splits[2], (N_SECTION, D, KVD), D ** -0.5, 0.0625, ((0, 16), (1, 16))),
        "value_weight": normal_values(splits[3], (N_SECTION, D, KVD), D ** -0.5, 0.0625, ((0, 16), (1, 16))),
        "query_gain": jnp.clip(0.5 + 1.5 * jax.random.uniform(splits[4], (N_SECTION, HD), jnp.float32) ** block_scale(splits[4], (N_SECTION, HD), ((0, 16),), -0.2, 0.2), 0.5, 2.0),
        "key_gain": jnp.clip(0.5 + 1.5 * jax.random.uniform(splits[5], (N_SECTION, HD), jnp.float32) ** block_scale(splits[5], (N_SECTION, HD), ((0, 16),), -0.2, 0.2), 0.5, 2.0),
        "tiles_seen": with_ends(jax.random.randint(splits[6], (TEXT,), 0, TILES + 1), jax.random.fold_in(splits[6], 1), 0, TILES).astype(jnp.int32),
        "context_grad": normal_values(splits[7], (N_SECTION, TEXT, QD), 1.0, 6.0, ((0, 16), (2, 16))),
    }


epsilon = 1e-05

def head_norm(raw_rows, gain_row):
    inverse = lax.rsqrt(lax.optimization_barrier(jnp.mean(raw_rows * raw_rows, -1, keepdims=True)) + epsilon)
    return (raw_rows * inverse * gain_row, inverse)

def head_norm_back(raw_rows, inverse, gain_row, upstream):
    scaled = upstream * gain_row
    return inverse * scaled - raw_rows * inverse ** 3 * lax.optimization_barrier(jnp.mean(raw_rows * scaled, -1, keepdims=True))

def section_pass(image_rows, visible, empty_row, queries, key_weight, value_weight, query_gain, key_gain, context_grad):
    score_scale = HD ** (-0.5)
    kv_weight = jnp.concatenate([key_weight, value_weight], 1)
    kv_raw = jnp.dot(image_rows, kv_weight, preferred_element_type=jnp.float32)
    key_raw = kv_raw[:, :KVD].reshape(IMG, KVH, HD)
    keys_float, key_inverse = head_norm(key_raw, key_gain)
    keys = keys_float.astype(jnp.bfloat16).astype(jnp.float32)
    values = kv_raw[:, KVD:].reshape(IMG, KVH, HD).astype(jnp.bfloat16).astype(jnp.float32)
    query_raw = queries.astype(jnp.float32).reshape(TEXT, KVH, GROUP, HD)
    normed_float, query_inverse = head_norm(query_raw, query_gain)
    normed = normed_float.astype(jnp.bfloat16).astype(jnp.float32)
    scores = jnp.einsum('tkgd,jkd->kgtj', normed, keys) * score_scale
    expo = jnp.where(visible, jnp.exp(scores), 0.0)
    totals = lax.optimization_barrier(jnp.sum(expo, -1, keepdims=True)) + empty_row
    probs = expo / totals
    probs_low = probs.astype(jnp.bfloat16).astype(jnp.float32)
    context = jnp.einsum('kgtj,jkd->tkgd', probs_low, values).astype(jnp.bfloat16).reshape(TEXT, QD)
    upstream = context_grad.astype(jnp.float32).reshape(TEXT, KVH, GROUP, HD)
    prob_grad = jnp.einsum('tkgd,jkd->kgtj', upstream, values)
    row_dot = lax.optimization_barrier(jnp.sum(probs * prob_grad, -1, keepdims=True))
    score_grad = (probs * (prob_grad - row_dot)).astype(jnp.bfloat16).astype(jnp.float32)
    normed_grad = jnp.einsum('kgtj,jkd->tkgd', score_grad, keys) * score_scale
    query_grad = head_norm_back(query_raw, query_inverse, query_gain, normed_grad).astype(jnp.bfloat16).reshape(TEXT, QD)
    key_grad = jnp.einsum('kgtj,tkgd->jkd', score_grad, normed) * score_scale
    value_grad = jnp.einsum('kgtj,tkgd->jkd', probs_low, upstream)
    key_raw_grad = head_norm_back(key_raw, key_inverse, key_gain, key_grad)
    kv_grad = jnp.concatenate([key_raw_grad.reshape(IMG, KVD), value_grad.reshape(IMG, KVD)], 1).astype(jnp.bfloat16)
    weight_grad = lax.dot_general(image_rows, kv_grad, (((0,), (0,)), ((), ())), preferred_element_type=jnp.float32).astype(jnp.bfloat16)
    image_term = lax.dot_general(kv_grad, kv_weight, (((1,), (1,)), ((), ())), preferred_element_type=jnp.float32)
    return (context, query_grad, weight_grad[:, :KVD], weight_grad[:, KVD:], image_term)

def reference(image_rows, queries, key_weight, value_weight, query_gain, key_gain, tiles_seen, context_grad):
    tile_index = jnp.arange(IMG, dtype=jnp.int32) // TILE_ROWS
    visible = tile_index[None, :] < tiles_seen[:, None]
    empty_row = (tiles_seen == 0).astype(jnp.float32)[:, None]

    def one_section(carry, stacked):
        context, query_grad, key_part, value_part, image_term = section_pass(image_rows, visible, empty_row, *stacked)
        return (carry + image_term, (context, query_grad, key_part, value_part))
    start_grad = jnp.zeros((IMG, D), jnp.float32)
    image_grad, outputs = lax.scan(one_section, start_grad, (queries, key_weight, value_weight, query_gain, key_gain, context_grad))
    return (outputs[0], outputs[1], outputs[2], outputs[3], image_grad)
```

```python
import jax
import jax.numpy as jnp
from jax import lax
from jax.sharding import PartitionSpec as P

TILE_ROWS = 96
CORES = 2
epsilon = 1e-05

f32 = jnp.float32
bf16 = jnp.bfloat16


def head_norm(raw_rows, gain_row):
    inverse = lax.rsqrt(jnp.mean(raw_rows * raw_rows, -1, keepdims=True) + epsilon)
    return (raw_rows * inverse * gain_row, inverse)


def head_norm_back(raw_rows, inverse, gain_row, upstream):
    scaled = upstream * gain_row
    return inverse * scaled - raw_rows * inverse**3 * jnp.mean(raw_rows * scaled, -1, keepdims=True)


def shards(
    image_rows, queries, key_weight, value_weight, query_gain, key_gain, tiles_seen, context_grad
):
    sections = lax.axis_size("section")
    tp = lax.axis_size("tp")
    chips = tp // CORES
    core = lax.axis_index("tp") % CORES
    same_core = [[i for i in range(tp) if i % CORES == c] for c in range(CORES)]
    swap = [(i, i ^ 1) for i in range(tp)]

    def other_core(x):
        return lax.ppermute(x, "tp", swap)

    def over_chips(x):
        return lax.all_to_all(x, "tp", 0, 0, axis_index_groups=same_core)

    own_rows, features = image_rows.shape
    half = sections * own_rows // CORES
    kv_width = key_weight.shape[2]
    head = query_gain.shape[1]
    kv_heads = kv_width // head
    text = queries.shape[1]
    heads = queries.shape[2] // head
    score_scale = head ** (-0.5)
    key_gain_row, query_gain_row = key_gain[0], query_gain[0]

    blocks = lax.all_to_all(
        jnp.broadcast_to(image_rows[None], (sections, own_rows, features)), "section", 0, 0
    )
    halves = blocks.reshape(CORES, half, features)
    rows_mine = lax.dynamic_index_in_dim(halves, core, 0, keepdims=False)
    rows_other = lax.dynamic_index_in_dim(halves, 1 - core, 0, keepdims=False)

    def project(rows):
        k = jnp.dot(rows, key_weight[0], preferred_element_type=f32)
        v = jnp.dot(rows, value_weight[0], preferred_element_type=f32)
        both = jnp.concatenate(
            [k.reshape(half, kv_heads, head), v.reshape(half, kv_heads, head)], -1
        )
        return both.transpose(1, 0, 2)

    received = other_core(project(rows_other).astype(bf16))
    partial = (project(rows_mine) + received.astype(f32)).astype(bf16)
    kv_raw = jnp.sum(over_chips(partial).astype(f32), 0)
    key_raw = kv_raw[:, :head]
    keys_float, key_inverse = head_norm(key_raw, key_gain_row)
    kv_mine = jnp.concatenate([keys_float, kv_raw[:, head:]], 1).astype(bf16)
    kv_all = jnp.concatenate([kv_mine, other_core(kv_mine)], 0)
    keys, values = kv_all[:, :head], kv_all[:, head:]

    query_raw = queries[0].reshape(text, heads, head).transpose(1, 0, 2).astype(f32)
    upstream = context_grad[0].reshape(text, heads, head).transpose(1, 0, 2)
    normed_float, query_inverse = head_norm(query_raw, query_gain_row)
    normed = normed_float.astype(bf16)
    local = jnp.arange(CORES * half, dtype=jnp.int32)
    row = jnp.where(local < half, local + core * half, local - core * half)
    visible = (row // TILE_ROWS)[None, :] < tiles_seen[:, None]
    empty_row = (tiles_seen == 0).astype(f32)[:, None]
    scores = jnp.einsum("htd,jd->htj", normed, keys, preferred_element_type=f32) * score_scale
    expo = jnp.where(visible, jnp.exp(scores), 0.0)
    totals = jnp.sum(expo, -1, keepdims=True) + empty_row
    probs = expo / totals
    probs_low = probs.astype(bf16)
    prob_grad = jnp.einsum("htd,jd->htj", upstream, values, preferred_element_type=f32)
    row_dot = jnp.sum(probs * prob_grad, -1, keepdims=True)
    score_grad = (probs * (prob_grad - row_dot)).astype(bf16)
    key_grad = jnp.einsum("htj,htd->jd", score_grad, normed, preferred_element_type=f32) * score_scale
    value_grad = jnp.einsum("htj,htd->jd", probs_low, upstream, preferred_element_type=f32)
    kv_grad_part = jnp.concatenate([key_grad, value_grad], 1)
    received = other_core(kv_grad_part[half:].astype(bf16))
    kv_grad_raw = kv_grad_part[:half] + received.astype(f32)
    key_raw_grad = head_norm_back(key_raw, key_inverse, key_gain_row, kv_grad_raw[:, :head])
    kv_grad = jnp.concatenate([key_raw_grad, kv_grad_raw[:, head:]], 1).astype(bf16)
    grads_mine = over_chips(jnp.broadcast_to(kv_grad[None], (chips, half, 2 * head)))
    grads_other = other_core(grads_mine)

    context = jnp.einsum("htj,jd->thd", probs_low, values, preferred_element_type=f32)
    context = context.astype(bf16).reshape(1, text, heads * head)
    normed_grad = (
        jnp.einsum("htj,jd->htd", score_grad, keys, preferred_element_type=f32) * score_scale
    )
    query_grad = head_norm_back(query_raw, query_inverse, query_gain_row, normed_grad)
    query_grad = query_grad.astype(bf16).transpose(1, 0, 2).reshape(1, text, heads * head)

    grads = jnp.concatenate([grads_mine, grads_other], 1).transpose(1, 0, 2)
    key_grads = grads[:, :, :head].reshape(CORES * half, kv_width)
    value_grads = grads[:, :, head:].reshape(CORES * half, kv_width)
    image_part = lax.dot_general(
        key_grads, key_weight[0], (((1,), (1,)), ((), ())), preferred_element_type=f32
    ) + lax.dot_general(
        value_grads, value_weight[0], (((1,), (1,)), ((), ())), preferred_element_type=f32
    )
    image_part = image_part.astype(bf16).reshape(CORES, half, features)
    image_part = jnp.where(core == 0, image_part, image_part[::-1])
    image_grad = lax.all_to_all(
        image_part.reshape(sections, own_rows, features), "section", 0, 0
    )
    image_grad = jnp.sum(image_grad.astype(f32), 0)
    image_local = jnp.concatenate([rows_mine, rows_other], 0)

    def weight_grad(column_grads):
        return lax.dot_general(
            image_local, column_grads, (((0,), (0,)), ((), ())), preferred_element_type=f32
        ).astype(bf16)[None]

    return (context, query_grad, weight_grad(key_grads), weight_grad(value_grads), image_grad)


def solution(mesh):
    return jax.shard_map(
        shards,
        mesh=mesh,
        in_specs=(
            P("section", "tp"),
            P("section", None, "tp"),
            P("section", "tp", None),
            P("section", "tp", None),
            P("section", None),
            P("section", None),
            P(),
            P("section", None, "tp"),
        ),
        out_specs=(
            P("section", None, "tp"),
            P("section", None, "tp"),
            P("section", "tp", None),
            P("section", "tp", None),
            P("section", "tp"),
        ),
        check_vma=False,
    )
```

```python
import functools

import jax
import jax.numpy as jnp
from jax import lax
from jax.experimental import pallas as pl
from jax.experimental.pallas import tpu as pltpu
from jax.sharding import PartitionSpec as P

TILE_ROWS = 96
CORES = 2
TEXT_STEP = 256
epsilon = 1e-05

f32 = jnp.float32
bf16 = jnp.bfloat16

BOTH_LAST = (((1,), (1,)), ((), ()))
BOTH_FIRST = (((0,), (0,)), ((), ()))

VMEM = pl.BlockSpec(memory_space=pltpu.VMEM)
SMEM = pl.BlockSpec(memory_space=pltpu.SMEM)
PARAMS = pltpu.CompilerParams(vmem_limit_bytes=40 * 1024 * 1024)


def dot(a, b, dims=(((1,), (0,)), ((), ()))):
    return lax.dot_general(a, b, dims, preferred_element_type=f32)


def head_norm(raw_rows, gain_row):
    inverse = lax.rsqrt(jnp.mean(raw_rows * raw_rows, -1, keepdims=True) + epsilon)
    return (raw_rows * inverse * gain_row, inverse)


def head_norm_back(raw_rows, inverse, gain_row, upstream):
    scaled = upstream * gain_row
    return inverse * scaled - raw_rows * (
        inverse * inverse * inverse * jnp.mean(raw_rows * scaled, -1, keepdims=True)
    )


def half_rows(ref, which, half):
    return ref[pl.ds(pl.multiple_of(which * half, half), half), :]


def project_kernel(add, core_ref, rows_ref, key_ref, value_ref, *refs):
    out_ref = refs[-1]
    kv_heads, half, width = out_ref.shape
    head = width // 2
    core = core_ref[0]
    rows = half_rows(rows_ref, core if add else 1 - core, half)
    for low in range(0, kv_heads, 2):
        for part, weight_ref in enumerate((key_ref, value_ref)):
            pair = dot(rows, weight_ref[:, low * head : (low + 2) * head])
            for i in range(2):
                here = pair[:, i * head : (i + 1) * head]
                where = slice(part * head, (part + 1) * head)
                if add:
                    here = here + refs[0][low + i, :, where].astype(f32)
                out_ref[low + i, :, where] = here.astype(bf16)


def norm_kernel(parts_ref, gain_ref, kv_ref, raw_ref):
    total = parts_ref[0].astype(f32)
    for i in range(1, parts_ref.shape[0]):
        total = total + parts_ref[i].astype(f32)
    head = gain_ref.shape[1]
    key_raw = total[:, :head]
    keys, _ = head_norm(key_raw, gain_ref[...])
    raw_ref[...] = key_raw
    kv_ref[:, :head] = keys.astype(bf16)
    kv_ref[:, head:] = total[:, head:].astype(bf16)


def attention_kernel(
    core_ref, mine_ref, other_ref, query_ref, up_ref, gain_ref, seen_ref,
    context_ref, query_grad_ref, send_ref, keep_ref,
):
    core = core_ref[0]
    head = gain_ref.shape[1]
    half = mine_ref.shape[0]
    text, width = query_ref.shape
    tiles_half = half // TILE_ROWS
    scale = head ** (-0.5)
    kv = jnp.concatenate([mine_ref[...], other_ref[...]], 0)
    keys, values = kv[:, :head], kv[:, head:]
    keys_t = keys.astype(f32).T.astype(bf16)
    values_t = values.astype(f32).T.astype(bf16)
    gain = gain_ref[...]
    key_grad = jnp.zeros((2 * half, head), f32)
    value_grad = jnp.zeros((2 * half, head), f32)
    for t in range(0, text, TEXT_STEP):
        now = slice(t, t + TEXT_STEP)
        seen = seen_ref[:, now]
        empty = jnp.where(seen == 0, 1.0, 0.0)
        shown = []
        for side in (core, 1 - core):
            for i in range(tiles_half):
                tile = side * tiles_half + i
                shown.append(jnp.broadcast_to(tile < seen, (TILE_ROWS, TEXT_STEP)))
        visible = jnp.concatenate(shown, 0)
        for h in range(width // head):
            cols = slice(h * head, (h + 1) * head)
            query = query_ref[now, cols].astype(f32)
            up = up_ref[now, cols]
            normed_float, inverse = head_norm(query, gain)
            normed = normed_float.astype(bf16)
            scores = dot(keys, normed, BOTH_LAST) * scale
            expo = jnp.where(visible, jnp.exp(scores), 0.0)
            totals = jnp.sum(expo, 0, keepdims=True) + empty
            probs = expo * (1.0 / totals)
            probs_low = probs.astype(bf16)
            prob_grad = dot(values, up, BOTH_LAST)
            row_dot = jnp.sum(probs * prob_grad, 0, keepdims=True)
            score_grad = (probs * (prob_grad - row_dot)).astype(bf16)
            key_grad = key_grad + dot(score_grad, normed)
            value_grad = value_grad + dot(probs_low, up)
            context_ref[now, cols] = dot(values_t, probs_low).T.astype(bf16)
            normed_grad = dot(keys_t, score_grad).T * scale
            query_grad_ref[now, cols] = head_norm_back(
                query, inverse, gain, normed_grad
            ).astype(bf16)
    key_grad = key_grad * scale
    keep_ref[:, :head] = key_grad[:half]
    keep_ref[:, head:] = value_grad[:half]
    send_ref[:, :head] = key_grad[half:].astype(bf16)
    send_ref[:, head:] = value_grad[half:].astype(bf16)


def kv_grad_kernel(keep_ref, received_ref, raw_ref, gain_ref, out_ref):
    total = keep_ref[...] + received_ref[...].astype(f32)
    gain = gain_ref[...]
    head = gain.shape[1]
    key_raw = raw_ref[...]
    _, inverse = head_norm(key_raw, gain)
    key_raw_grad = head_norm_back(key_raw, inverse, gain, total[:, :head]).astype(bf16)
    value_grad = total[:, head:].astype(bf16)
    for i in range(out_ref.shape[0]):
        out_ref[i, :, :head] = key_raw_grad
        out_ref[i, :, head:] = value_grad


def image_product(grads_ref, key_ref, value_ref):
    kv_heads, half, width = grads_ref.shape
    head = width // 2
    total = None
    for h in range(kv_heads):
        cols = slice(h * head, (h + 1) * head)
        weight = jnp.concatenate([key_ref[:, cols], value_ref[:, cols]], 1)
        term = dot(grads_ref[h], weight, BOTH_LAST)
        total = term if total is None else total + term
    return total.astype(bf16)


def image_kernel(grads_ref, key_ref, value_ref, out_ref):
    out_ref[...] = image_product(grads_ref, key_ref, value_ref)


def image_both_kernel(core_ref, grads_ref, key_ref, value_ref, mine_ref, out_ref):
    half = mine_ref.shape[0]
    core = core_ref[0]
    out_ref[pl.ds(pl.multiple_of(core * half, half), half), :] = mine_ref[...]
    out_ref[pl.ds(pl.multiple_of((1 - core) * half, half), half), :] = image_product(
        grads_ref, key_ref, value_ref
    )


def weight_grad_kernel(core_ref, rows_ref, mine_ref, other_ref, key_ref, value_ref):
    kv_heads, half, width = mine_ref.shape
    head = width // 2
    core = core_ref[0]
    rows_mine = half_rows(rows_ref, core, half).astype(f32).T.astype(bf16)
    rows_other = half_rows(rows_ref, 1 - core, half).astype(f32).T.astype(bf16)
    for h in range(kv_heads):
        cols = slice(h * head, (h + 1) * head)
        both = (dot(rows_mine, mine_ref[h]) + dot(rows_other, other_ref[h])).astype(bf16)
        key_ref[:, cols] = both[:, :head]
        value_ref[:, cols] = both[:, head:]


def call(kernel, outs, *args, scalar=False):
    many = len(outs) > 1
    shapes = tuple(jax.ShapeDtypeStruct(shape, kind) for shape, kind in outs)
    return pl.pallas_call(
        kernel,
        out_shape=shapes if many else shapes[0],
        in_specs=[SMEM if scalar and i == 0 else VMEM for i in range(len(args))],
        out_specs=(VMEM,) * len(outs) if many else VMEM,
        compiler_params=PARAMS,
    )(*args)


def fence(*arrays):
    return lax.optimization_barrier(arrays)


def shards(
    image_rows, queries, key_weight, value_weight, query_gain, key_gain, tiles_seen, context_grad
):
    sections = lax.axis_size("section")
    tp = lax.axis_size("tp")
    chips = tp // CORES
    core = (lax.axis_index("tp") % CORES).astype(jnp.int32).reshape(1)
    same_core = [[i for i in range(tp) if i % CORES == c] for c in range(CORES)]
    swap = [(i, i ^ 1) for i in range(tp)]

    def other_core(x):
        return lax.ppermute(x, "tp", swap)

    def over_chips(x):
        return lax.all_to_all(x, "tp", 0, 0, axis_index_groups=same_core)

    own_rows, features = image_rows.shape
    rows_total = sections * own_rows
    half = rows_total // CORES
    kv_width = key_weight.shape[2]
    head = query_gain.shape[1]
    kv_heads = kv_width // head
    text, width = queries.shape[1:]
    pieces = (kv_heads, half, 2 * head)

    blocks = lax.all_to_all(
        jnp.broadcast_to(image_rows[None], (sections, own_rows, features)), "section", 0, 0
    )
    blocks, key_weight, value_weight, queries, context_grad = fence(
        blocks, key_weight[0], value_weight[0], queries[0], context_grad[0]
    )
    rows = blocks.reshape(rows_total, features)
    for_other = call(
        functools.partial(project_kernel, False), [(pieces, bf16)],
        core, rows, key_weight, value_weight, scalar=True,
    )
    received = other_core(for_other)
    partial = call(
        functools.partial(project_kernel, True), [(pieces, bf16)],
        core, rows, key_weight, value_weight, received, scalar=True,
    )
    parts = over_chips(partial)
    kv_mine, key_raw = call(
        norm_kernel, [((half, 2 * head), bf16), ((half, head), f32)], parts, key_gain
    )
    kv_other = other_core(kv_mine)
    context, query_grad, send, keep = call(
        attention_kernel,
        [
            ((text, width), bf16),
            ((text, width), bf16),
            ((half, 2 * head), bf16),
            ((half, 2 * head), f32),
        ],
        core, kv_mine, kv_other, queries, context_grad, query_gain, tiles_seen[None],
        scalar=True,
    )
    received = other_core(send)
    copies = call(kv_grad_kernel, [(pieces, bf16)], keep, received, key_raw, key_gain)
    grads_mine = over_chips(copies)
    grads_other = other_core(grads_mine)
    image_mine = call(
        image_kernel, [((half, features), bf16)], grads_mine, key_weight, value_weight
    )
    image_part = call(
        image_both_kernel, [((rows_total, features), bf16)],
        core, grads_other, key_weight, value_weight, image_mine, scalar=True,
    )
    image_parts = lax.all_to_all(
        image_part.reshape(sections, own_rows, features), "section", 0, 0
    )
    image_parts, rows, grads_mine, grads_other = fence(image_parts, rows, grads_mine, grads_other)
    image_grad = jnp.sum(image_parts.astype(f32), 0)
    key_weight_grad, value_weight_grad = call(
        weight_grad_kernel, [((features, kv_width), bf16)] * 2,
        core, rows, grads_mine, grads_other, scalar=True,
    )
    return (
        context[None], query_grad[None], key_weight_grad[None], value_weight_grad[None], image_grad
    )


def solution(mesh):
    return jax.shard_map(
        shards,
        mesh=mesh,
        in_specs=(
            P("section", "tp"),
            P("section", None, "tp"),
            P("section", "tp", None),
            P("section", "tp", None),
            P("section", None),
            P("section", None),
            P(),
            P("section", None, "tp"),
        ),
        out_specs=(
            P("section", None, "tp"),
            P("section", None, "tp"),
            P("section", "tp", None),
            P("section", "tp", None),
            P("section", "tp"),
        ),
        check_vma=False,
    )
```

```python
import functools

import jax
import jax.numpy as jnp
from jax import lax
from jax.experimental import pallas as pl
from jax.experimental.pallas import tpu as pltpu
from jax.sharding import PartitionSpec as P

TILE_ROWS = 96
CORES = 2
IMAGE_STEPS = 2
LOG2_E = 1.4426950408889634
epsilon = 1e-05

f32 = jnp.float32
bf16 = jnp.bfloat16

BOTH_LAST = (((1,), (1,)), ((), ()))
BOTH_FIRST = (((0,), (0,)), ((), ()))

ANY = pl.BlockSpec(memory_space=pl.ANY)
VMEM = pl.BlockSpec(memory_space=pltpu.VMEM)
SMEM = pl.BlockSpec(memory_space=pltpu.SMEM)
PARAMS = pltpu.CompilerParams(vmem_limit_bytes=40 * 1024 * 1024)


def dot(a, b, dims=(((1,), (0,)), ((), ()))):
    return lax.dot_general(a, b, dims, preferred_element_type=f32)


def head_norm(raw_rows, gain_row):
    inverse = lax.rsqrt(jnp.mean(raw_rows * raw_rows, -1, keepdims=True) + epsilon)
    return (raw_rows * inverse * gain_row, inverse)


def head_norm_back(raw_rows, inverse, gain_row, upstream):
    scaled = upstream * gain_row
    return inverse * scaled - raw_rows * (
        inverse * inverse * inverse * jnp.mean(raw_rows * scaled, -1, keepdims=True)
    )


def half_rows(ref, which, half):
    return ref[pl.ds(pl.multiple_of(which * half, half), half), :]


def copies_kernel(rows_ref, out_ref):
    for i in range(out_ref.shape[0]):
        out_ref[i] = rows_ref[...]


def project_kernel(add, core_ref, rows_ref, key_ref, value_ref, *refs):
    out_ref = refs[-1]
    kv_heads, half, width = out_ref.shape
    head = width // 2
    core = core_ref[0]
    rows = half_rows(rows_ref, core if add else 1 - core, half)
    for low in range(0, kv_heads, 2):
        for part, weight_ref in enumerate((key_ref, value_ref)):
            pair = dot(rows, weight_ref[:, low * head : (low + 2) * head])
            for i in range(2):
                here = pair[:, i * head : (i + 1) * head]
                where = slice(part * head, (part + 1) * head)
                if add:
                    here = here + refs[0][low + i, :, where].astype(f32)
                out_ref[low + i, :, where] = here.astype(bf16)


def norm_kernel(parts_ref, gain_ref, kv_ref, raw_ref):
    total = parts_ref[0].astype(f32)
    for i in range(1, parts_ref.shape[0]):
        total = total + parts_ref[i].astype(f32)
    head = gain_ref.shape[1]
    key_raw = total[:, :head]
    keys, _ = head_norm(key_raw, gain_ref[...])
    raw_ref[...] = key_raw
    kv_ref[:, :head] = keys.astype(bf16)
    kv_ref[:, head:] = total[:, head:].astype(bf16)


def attention_kernel(
    core_ref, mine_ref, other_ref, query_ref, up_ref, gain_ref, seen_ref,
    context_ref, query_grad_ref, send_ref, keep_ref,
    context_held, query_grad_held, sems,
):
    core = core_ref[0]
    head = gain_ref.shape[1]
    half = mine_ref.shape[0]
    text, width = query_ref.shape
    tiles_half = half // TILE_ROWS
    scale = head ** (-0.5)
    kv = jnp.concatenate([mine_ref[...], other_ref[...]], 0)
    keys, values = kv[:, :head], kv[:, head:]
    keys_t = keys.astype(f32).T.astype(bf16)
    values_t = values.astype(f32).T.astype(bf16)
    gain = gain_ref[...]
    seen = seen_ref[...]
    empty = jnp.where(seen == 0, 1.0, 0.0)
    shown = []
    for side in (core, 1 - core):
        for i in range(tiles_half):
            shown.append(jnp.broadcast_to(side * tiles_half + i < seen, (TILE_ROWS, text)))
    visible = jnp.concatenate(shown, 0)
    key_grad = jnp.zeros((2 * half, head), f32)
    value_grad = jnp.zeros((2 * half, head), f32)
    copies = []
    for h in range(width // head):
        cols = slice(h * head, (h + 1) * head)
        query = query_ref[:, cols].astype(f32)
        up = up_ref[:, cols]
        normed_float, inverse = head_norm(query, gain)
        normed = normed_float.astype(bf16)
        scores = dot(keys, normed, BOTH_LAST)
        expo = jnp.where(visible, jnp.exp2(scores * (scale * LOG2_E)), 0.0)
        totals = jnp.sum(expo, 0, keepdims=True) + empty
        probs = expo * (1.0 / totals)
        probs_low = probs.astype(bf16)
        prob_grad = dot(values, up, BOTH_LAST)
        row_dot = jnp.sum(probs * prob_grad, 0, keepdims=True)
        score_grad = (probs * (prob_grad - row_dot)).astype(bf16)
        key_grad = key_grad + dot(score_grad, normed)
        value_grad = value_grad + dot(probs_low, up)
        context_held[:, cols] = dot(values_t, probs_low).T.astype(bf16)
        normed_grad = dot(keys_t, score_grad).T * scale
        query_grad_held[:, cols] = head_norm_back(query, inverse, gain, normed_grad).astype(bf16)
        for i, (held, out) in enumerate(
            ((context_held, context_ref), (query_grad_held, query_grad_ref))
        ):
            copy = pltpu.make_async_copy(held.at[:, cols], out.at[:, cols], sems.at[2 * h + i])
            copy.start()
            copies.append(copy)
    key_grad = key_grad * scale
    keep_ref[:, :head] = key_grad[:half]
    keep_ref[:, head:] = value_grad[:half]
    send_ref[:, :head] = key_grad[half:].astype(bf16)
    send_ref[:, head:] = value_grad[half:].astype(bf16)
    for copy in copies:
        copy.wait()


def kv_grad_kernel(keep_ref, received_ref, raw_ref, gain_ref, out_ref):
    total = keep_ref[...] + received_ref[...].astype(f32)
    gain = gain_ref[...]
    head = gain.shape[1]
    key_raw = raw_ref[...]
    _, inverse = head_norm(key_raw, gain)
    key_raw_grad = head_norm_back(key_raw, inverse, gain, total[:, :head]).astype(bf16)
    value_grad = total[:, head:].astype(bf16)
    for i in range(out_ref.shape[0]):
        out_ref[i, :, :head] = key_raw_grad
        out_ref[i, :, head:] = value_grad


def image_product(grads_ref, key_ref, value_ref, now):
    kv_heads, half, width = grads_ref.shape
    head = width // 2
    total = None
    for h in range(kv_heads):
        cols = slice(h * head, (h + 1) * head)
        weight = jnp.concatenate([key_ref[now, cols], value_ref[now, cols]], 1)
        term = dot(grads_ref[h], weight, BOTH_LAST)
        total = term if total is None else total + term
    return total.astype(bf16)


def image_kernel(grads_ref, key_ref, value_ref, out_ref):
    out_ref[...] = image_product(grads_ref, key_ref, value_ref, slice(None))


def image_both_kernel(core_ref, grads_ref, key_ref, value_ref, mine_ref, out_ref, held, sems):
    half, features = mine_ref.shape
    core = core_ref[0]
    here = pl.ds(pl.multiple_of(core * half, half), half)
    there = pl.ds(pl.multiple_of((1 - core) * half, half), half)
    copies = [pltpu.make_async_copy(mine_ref, out_ref.at[here, :], sems.at[0])]
    copies[0].start()
    step = features // IMAGE_STEPS
    for i in range(IMAGE_STEPS):
        now = slice(i * step, (i + 1) * step)
        held[:, now] = image_product(grads_ref, key_ref, value_ref, now)
        copies.append(
            pltpu.make_async_copy(held.at[:, now], out_ref.at[there, now], sems.at[i + 1])
        )
        copies[-1].start()
    for copy in copies:
        copy.wait()


def weight_grad_kernel(core_ref, rows_ref, mine_ref, other_ref, key_ref, value_ref):
    kv_heads, half, width = mine_ref.shape
    head = width // 2
    core = core_ref[0]
    rows_mine = half_rows(rows_ref, core, half).astype(f32).T.astype(bf16)
    rows_other = half_rows(rows_ref, 1 - core, half).astype(f32).T.astype(bf16)
    for h in range(kv_heads):
        cols = slice(h * head, (h + 1) * head)
        both = (dot(rows_mine, mine_ref[h]) + dot(rows_other, other_ref[h])).astype(bf16)
        key_ref[:, cols] = both[:, :head]
        value_ref[:, cols] = both[:, head:]


def call(kernel, outs, *args, scalar=False, cost=None, scratch=(), to_hbm=()):
    many = len(outs) > 1
    shapes = tuple(jax.ShapeDtypeStruct(shape, kind) for shape, kind in outs)
    places = tuple(ANY if i in to_hbm else VMEM for i in range(len(outs)))
    return pl.pallas_call(
        kernel,
        out_shape=shapes if many else shapes[0],
        in_specs=[SMEM if scalar and i == 0 else VMEM for i in range(len(args))],
        out_specs=places if many else places[0],
        scratch_shapes=list(scratch),
        compiler_params=PARAMS,
        cost_estimate=cost,
    )(*args)


def fence(*arrays):
    return lax.optimization_barrier(arrays)


def shards(
    image_rows, queries, key_weight, value_weight, query_gain, key_gain, tiles_seen, context_grad
):
    sections = lax.axis_size("section")
    tp = lax.axis_size("tp")
    chips = tp // CORES
    core = (lax.axis_index("tp") % CORES).astype(jnp.int32).reshape(1)
    same_core = [[i for i in range(tp) if i % CORES == c] for c in range(CORES)]
    swap = [(i, i ^ 1) for i in range(tp)]

    def other_core(x):
        return lax.ppermute(x, "tp", swap)

    def over_chips(x):
        return lax.all_to_all(x, "tp", 0, 0, axis_index_groups=same_core)

    own_rows, features = image_rows.shape
    rows_total = sections * own_rows
    half = rows_total // CORES
    kv_width = key_weight.shape[2]
    head = query_gain.shape[1]
    kv_heads = kv_width // head
    text, width = queries.shape[1:]
    pieces = (kv_heads, half, 2 * head)

    image_rows, core = fence(image_rows, core)
    copies = call(
        copies_kernel, [((sections, own_rows, features), bf16)], image_rows,
        cost=pl.CostEstimate(flops=2**34, bytes_accessed=2**25, transcendentals=0),
    )
    blocks = lax.all_to_all(copies, "section", 0, 0)
    blocks, key_weight, value_weight, queries, context_grad = fence(
        blocks, key_weight[0], value_weight[0], queries[0], context_grad[0]
    )
    rows = blocks.reshape(rows_total, features)
    for_other = call(
        functools.partial(project_kernel, False), [(pieces, bf16)],
        core, rows, key_weight, value_weight, scalar=True,
    )
    received = other_core(for_other)
    partial = call(
        functools.partial(project_kernel, True), [(pieces, bf16)],
        core, rows, key_weight, value_weight, received, scalar=True,
    )
    parts = over_chips(partial)
    kv_mine, key_raw = call(
        norm_kernel, [((half, 2 * head), bf16), ((half, head), f32)], parts, key_gain
    )
    kv_other = other_core(kv_mine)
    context, query_grad, send, keep = call(
        attention_kernel,
        [
            ((text, width), bf16),
            ((text, width), bf16),
            ((half, 2 * head), bf16),
            ((half, 2 * head), f32),
        ],
        core, kv_mine, kv_other, queries, context_grad, query_gain, tiles_seen[None],
        scalar=True, to_hbm=(0, 1),
        scratch=[pltpu.VMEM((text, width), bf16)] * 2
        + [pltpu.SemaphoreType.DMA((2 * width // head,))],
    )
    received = other_core(send)
    copies = call(kv_grad_kernel, [(pieces, bf16)], keep, received, key_raw, key_gain)
    grads_mine = over_chips(copies)
    grads_other = other_core(grads_mine)
    image_mine = call(
        image_kernel, [((half, features), bf16)], grads_mine, key_weight, value_weight
    )
    image_part = call(
        image_both_kernel, [((rows_total, features), bf16)],
        core, grads_other, key_weight, value_weight, image_mine, scalar=True, to_hbm=(0,),
        scratch=[pltpu.VMEM((half, features), bf16), pltpu.SemaphoreType.DMA((IMAGE_STEPS + 1,))],
    )
    image_part, rows, grads_mine, grads_other = fence(image_part, rows, grads_mine, grads_other)
    image_parts = lax.all_to_all(
        image_part.reshape(sections, own_rows, features), "section", 0, 0
    )
    key_weight_grad, value_weight_grad = call(
        weight_grad_kernel, [((features, kv_width), bf16)] * 2,
        core, rows, grads_mine, grads_other, scalar=True,
        cost=pl.CostEstimate(
            flops=2 * features * 2 * kv_width * rows_total,
            bytes_accessed=4 * features * 2 * kv_width,
            transcendentals=0,
        ),
    )
    image_parts, key_weight_grad, value_weight_grad = fence(
        image_parts, key_weight_grad, value_weight_grad
    )
    image_grad = jnp.sum(image_parts.astype(f32), 0)
    return (
        context[None], query_grad[None], key_weight_grad[None], value_weight_grad[None], image_grad
    )


def solution(mesh):
    return jax.shard_map(
        shards,
        mesh=mesh,
        in_specs=(
            P("section", "tp"),
            P("section", None, "tp"),
            P("section", "tp", None),
            P("section", "tp", None),
            P("section", None),
            P("section", None),
            P(),
            P("section", None, "tp"),
        ),
        out_specs=(
            P("section", None, "tp"),
            P("section", None, "tp"),
            P("section", "tp", None),
            P("section", "tp", None),
            P("section", "tp"),
        ),
        check_vma=False,
    )
```

```python
import jax
import jax.numpy as jnp
from jax import lax
from jax.experimental import pallas as pl
from jax.experimental.pallas import tpu as pltpu
from jax.sharding import PartitionSpec as P

TILE_ROWS = 96
CORES = 2
LOG2_E = 1.4426950408889634
epsilon = 1e-05

f32 = jnp.float32
bf16 = jnp.bfloat16

BOTH_LAST = (((1,), (1,)), ((), ()))

ANY = pl.BlockSpec(memory_space=pl.ANY)
VMEM = pl.BlockSpec(memory_space=pltpu.VMEM)
SMEM = pl.BlockSpec(memory_space=pltpu.SMEM)
PARAMS = pltpu.CompilerParams(vmem_limit_bytes=40 * 1024 * 1024)


def dot(a, b, dims=(((1,), (0,)), ((), ()))):
    return lax.dot_general(a, b, dims, preferred_element_type=f32)


def head_norm(raw_rows, gain_row):
    inverse = lax.rsqrt(jnp.mean(raw_rows * raw_rows, -1, keepdims=True) + epsilon)
    return (raw_rows * inverse * gain_row, inverse)


def head_norm_back(raw_rows, inverse, gain_row, upstream):
    scaled = upstream * gain_row
    return inverse * scaled - raw_rows * (
        inverse * inverse * inverse * jnp.mean(raw_rows * scaled, -1, keepdims=True)
    )


def by_core(core, zero, one):
    return jnp.where(core == 0, zero, one)


def copies_kernel(rows_ref, out_ref):
    for i in range(out_ref.shape[0]):
        out_ref[i] = rows_ref[...]


def project_kernel(core_ref, rows_ref, key_ref, value_ref, *refs):
    *before, out_ref = refs
    kv_heads, _, head = out_ref.shape
    rows = rows_ref[...]
    for kind, weight_ref in enumerate((key_ref, value_ref)):

        @pl.when(core_ref[0] == kind)
        def _(weight_ref=weight_ref):
            for low in range(0, kv_heads, 2):
                pair = dot(rows, weight_ref[:, low * head : (low + 2) * head])
                for i in range(2):
                    here = pair[:, i * head : (i + 1) * head]
                    if before:
                        here = here + before[0][low + i]
                    out_ref[low + i] = here.astype(out_ref.dtype)


def norm_kernel(core_ref, parts_ref, gain_ref, kv_ref, raw_ref):
    total = parts_ref[0].astype(f32)
    for i in range(1, parts_ref.shape[0]):
        total = total + parts_ref[i].astype(f32)
    keys, _ = head_norm(total, gain_ref[...])
    raw_ref[...] = total
    kv_ref[...] = by_core(core_ref[0], keys, total).astype(bf16)


def attention_kernel(
    core_ref, mine_ref, other_ref, query_ref, up_ref, gain_ref, seen_ref,
    context_ref, query_grad_ref, send_ref, keep_ref,
    context_held, query_grad_held, sems,
):
    core = core_ref[0]
    head = gain_ref.shape[1]
    rows = mine_ref.shape[0]
    text, width = query_ref.shape
    scale = head ** (-0.5)
    keys = by_core(core, mine_ref[...], other_ref[...])
    values = by_core(core, other_ref[...], mine_ref[...])
    keys_t = keys.astype(f32).T.astype(bf16)
    values_t = values.astype(f32).T.astype(bf16)
    gain = gain_ref[...]
    seen = seen_ref[...]
    empty = jnp.where(seen == 0, 1.0, 0.0)
    visible = jnp.concatenate(
        [jnp.broadcast_to(i < seen, (TILE_ROWS, text)) for i in range(rows // TILE_ROWS)], 0
    )
    key_grad = jnp.zeros((rows, head), f32)
    value_grad = jnp.zeros((rows, head), f32)
    copies = []
    for h in range(width // head):
        cols = slice(h * head, (h + 1) * head)
        query = query_ref[:, cols].astype(f32)
        up = up_ref[:, cols]
        normed_float, inverse = head_norm(query, gain)
        normed = normed_float.astype(bf16)
        scores = dot(keys, normed, BOTH_LAST)
        expo = jnp.where(visible, jnp.exp2(scores * (scale * LOG2_E)), 0.0)
        totals = jnp.sum(expo, 0, keepdims=True) + empty
        probs = expo * (1.0 / totals)
        probs_low = probs.astype(bf16)
        prob_grad = dot(values, up, BOTH_LAST)
        row_dot = jnp.sum(probs * prob_grad, 0, keepdims=True)
        score_grad = (probs * (prob_grad - row_dot)).astype(bf16)
        key_grad = key_grad + dot(score_grad, normed)
        value_grad = value_grad + dot(probs_low, up)
        context_held[:, cols] = dot(values_t, probs_low).T.astype(bf16)
        normed_grad = dot(keys_t, score_grad).T * scale
        query_grad_held[:, cols] = head_norm_back(query, inverse, gain, normed_grad).astype(bf16)
        for i, (held, out) in enumerate(
            ((context_held, context_ref), (query_grad_held, query_grad_ref))
        ):
            copy = pltpu.make_async_copy(held.at[:, cols], out.at[:, cols], sems.at[2 * h + i])
            copy.start()
            copies.append(copy)
    key_grad = key_grad * scale
    keep_ref[...] = by_core(core, key_grad, value_grad)
    send_ref[...] = by_core(core, value_grad, key_grad).astype(bf16)
    for copy in copies:
        copy.wait()


def kv_grad_kernel(core_ref, keep_ref, received_ref, raw_ref, gain_ref, out_ref):
    total = keep_ref[...] + received_ref[...].astype(f32)
    gain = gain_ref[...]
    raw = raw_ref[...]
    _, inverse = head_norm(raw, gain)
    key_raw_grad = head_norm_back(raw, inverse, gain, total)
    kv_grad = by_core(core_ref[0], key_raw_grad, total).astype(bf16)
    for i in range(out_ref.shape[0]):
        out_ref[i] = kv_grad


def image_product(grads_ref, weight_ref, now):
    kv_heads, _, head = grads_ref.shape
    total = None
    for low in range(0, kv_heads, 2):
        pair = jnp.concatenate([grads_ref[low], grads_ref[low + 1]], 1)
        term = dot(pair, weight_ref[now, low * head : (low + 2) * head], BOTH_LAST)
        total = term if total is None else total + term
    return total


def image_kernel(core_ref, grads_ref, key_ref, value_ref, out_ref):
    for kind, weight_ref in enumerate((key_ref, value_ref)):

        @pl.when(core_ref[0] == kind)
        def _(weight_ref=weight_ref):
            out_ref[...] = image_product(grads_ref, weight_ref, slice(None)).astype(out_ref.dtype)


def add_kernel(own_ref, received_ref, out_ref):
    out_ref[...] = (own_ref[...] + received_ref[...].astype(f32)).astype(bf16)


def weight_grad_kernel(core_ref, rows_ref, mine_ref, other_ref, key_ref, value_ref):
    kv_heads, _, head = mine_ref.shape
    core = core_ref[0]
    rows_t = rows_ref[...].astype(f32).T.astype(bf16)
    for low in range(0, kv_heads, 2):
        cols = slice(low * head, (low + 2) * head)
        mine = jnp.concatenate([mine_ref[low], mine_ref[low + 1]], 1)
        other = jnp.concatenate([other_ref[low], other_ref[low + 1]], 1)
        key_ref[:, cols] = dot(rows_t, by_core(core, mine, other)).astype(bf16)
        value_ref[:, cols] = dot(rows_t, by_core(core, other, mine)).astype(bf16)


def call(kernel, outs, *args, scalar=False, cost=None, scratch=(), to_hbm=()):
    many = len(outs) > 1
    shapes = tuple(jax.ShapeDtypeStruct(shape, kind) for shape, kind in outs)
    places = tuple(ANY if i in to_hbm else VMEM for i in range(len(outs)))
    return pl.pallas_call(
        kernel,
        out_shape=shapes if many else shapes[0],
        in_specs=[SMEM if scalar and i == 0 else VMEM for i in range(len(args))],
        out_specs=places if many else places[0],
        scratch_shapes=list(scratch),
        compiler_params=PARAMS,
        cost_estimate=cost,
    )(*args)


def fence(*arrays):
    return lax.optimization_barrier(arrays)


def shards(
    image_rows, queries, key_weight, value_weight, query_gain, key_gain, tiles_seen, context_grad
):
    sections = lax.axis_size("section")
    tp = lax.axis_size("tp")
    chips = tp // CORES
    core = (lax.axis_index("tp") % CORES).astype(jnp.int32).reshape(1)
    same_core = [[i for i in range(tp) if i % CORES == c] for c in range(CORES)]
    swap = [(i, i ^ 1) for i in range(tp)]

    def other_core(x):
        return lax.ppermute(x, "tp", swap)

    def to_core(x, c):
        return lax.ppermute(x, "tp", [(i ^ 1, i) for i in range(tp) if i % CORES == c])

    def over_chips(x):
        return lax.all_to_all(x, "tp", 0, 0, axis_index_groups=same_core)

    own_rows, features = image_rows.shape
    rows_total = sections * own_rows
    kv_width = key_weight.shape[2]
    head = query_gain.shape[1]
    kv_heads = kv_width // head
    text, width = queries.shape[1:]
    pieces = (kv_heads, rows_total, head)
    square = (rows_total, head)

    key_other = to_core(key_weight[0], 0)
    value_other = to_core(value_weight[0], 1)
    image_rows, core = fence(image_rows, core)
    copies = call(
        copies_kernel, [((sections, own_rows, features), bf16)], image_rows,
        cost=pl.CostEstimate(flops=2**34, bytes_accessed=2**25, transcendentals=0),
    )
    blocks = lax.all_to_all(copies, "section", 0, 0)
    blocks, key_weight, value_weight, key_other, value_other, queries, context_grad = fence(
        blocks, key_weight[0], value_weight[0], key_other, value_other, queries[0], context_grad[0]
    )
    rows = blocks.reshape(rows_total, features)
    rows_other = other_core(rows)
    partial = call(
        project_kernel, [(pieces, f32)], core, rows, key_weight, value_weight, scalar=True
    )
    partial = call(
        project_kernel, [(pieces, bf16)],
        core, rows_other, key_other, value_other, partial, scalar=True,
    )
    parts = over_chips(partial)
    kv_mine, raw = call(
        norm_kernel, [(square, bf16), (square, f32)], core, parts, key_gain, scalar=True
    )
    kv_other = other_core(kv_mine)
    context, query_grad, send, keep = call(
        attention_kernel,
        [((text, width), bf16), ((text, width), bf16), (square, bf16), (square, f32)],
        core, kv_mine, kv_other, queries, context_grad, query_gain, tiles_seen[None],
        scalar=True, to_hbm=(0, 1),
        scratch=[pltpu.VMEM((text, width), bf16)] * 2
        + [pltpu.SemaphoreType.DMA((2 * width // head,))],
    )
    received = other_core(send)
    copies = call(
        kv_grad_kernel, [(pieces, bf16)], core, keep, received, raw, key_gain, scalar=True
    )
    grads = over_chips(copies)
    image_send = call(
        image_kernel, [((rows_total, features), bf16)],
        core, grads, key_other, value_other, scalar=True,
    )
    received = other_core(image_send)
    image_own = call(
        image_kernel, [((rows_total, features), f32)],
        core, grads, key_weight, value_weight, scalar=True,
    )
    image_part = call(add_kernel, [((rows_total, features), bf16)], image_own, received)
    image_part, rows, grads = fence(image_part, rows, grads)
    grads_other = other_core(grads)
    image_parts = lax.all_to_all(
        image_part.reshape(sections, own_rows, features), "section", 0, 0
    )
    key_weight_grad, value_weight_grad = call(
        weight_grad_kernel, [((features, kv_width), bf16)] * 2,
        core, rows, grads, grads_other, scalar=True,
        cost=pl.CostEstimate(
            flops=2 * features * 2 * kv_width * rows_total,
            bytes_accessed=4 * features * 2 * kv_width,
            transcendentals=0,
        ),
    )
    image_parts, key_weight_grad, value_weight_grad = fence(
        image_parts, key_weight_grad, value_weight_grad
    )
    image_grad = jnp.sum(image_parts.astype(f32), 0)
    return (
        context[None], query_grad[None], key_weight_grad[None], value_weight_grad[None], image_grad
    )


def solution(mesh):
    return jax.shard_map(
        shards,
        mesh=mesh,
        in_specs=(
            P("section", "tp"),
            P("section", None, "tp"),
            P("section", "tp", None),
            P("section", "tp", None),
            P("section", None),
            P("section", None),
            P(),
            P("section", None, "tp"),
        ),
        out_specs=(
            P("section", None, "tp"),
            P("section", None, "tp"),
            P("section", "tp", None),
            P("section", "tp", None),
            P("section", "tp"),
        ),
        check_vma=False,
    )
```

```python
import jax
import jax.numpy as jnp
from jax import lax
from jax.experimental import pallas as pl
from jax.experimental.pallas import tpu as pltpu
from jax.sharding import PartitionSpec as P

TILE_ROWS = 96
CORES = 2
ADD_STEPS = 4
LOG2_E = 1.4426950408889634
epsilon = 1e-05

f32 = jnp.float32
bf16 = jnp.bfloat16

BOTH_LAST = (((1,), (1,)), ((), ()))

ANY = pl.BlockSpec(memory_space=pl.ANY)
HBM = pl.BlockSpec(memory_space=pltpu.HBM)
VMEM = pl.BlockSpec(memory_space=pltpu.VMEM)
SMEM = pl.BlockSpec(memory_space=pltpu.SMEM)
PARAMS = pltpu.CompilerParams(vmem_limit_bytes=16 * 1024 * 1024)


def dot(a, b, dims=(((1,), (0,)), ((), ()))):
    return lax.dot_general(a, b, dims, preferred_element_type=f32)


def head_norm(raw_rows, gain_row):
    inverse = lax.rsqrt(jnp.mean(raw_rows * raw_rows, -1, keepdims=True) + epsilon)
    return (raw_rows * inverse * gain_row, inverse)


def head_norm_back(raw_rows, inverse, gain_row, upstream):
    scaled = upstream * gain_row
    return inverse * scaled - raw_rows * (
        inverse * inverse * inverse * jnp.mean(raw_rows * scaled, -1, keepdims=True)
    )


def by_core(core, zero, one):
    return jnp.where(core == 0, zero, one)


def copies_kernel(rows_ref, out_ref):
    for i in range(out_ref.shape[0]):
        out_ref[i] = rows_ref[...]


def project_kernel(core_ref, rows_ref, key_ref, value_ref, *refs):
    *before, out_ref = refs
    kv_heads, _, head = out_ref.shape
    rows = rows_ref[...]
    for kind, weight_ref in enumerate((key_ref, value_ref)):

        @pl.when(core_ref[0] == kind)
        def _(weight_ref=weight_ref):
            for low in range(0, kv_heads, 2):
                pair = dot(rows, weight_ref[:, low * head : (low + 2) * head])
                for i in range(2):
                    here = pair[:, i * head : (i + 1) * head]
                    if before:
                        here = here + before[0][low + i]
                    out_ref[low + i] = here.astype(out_ref.dtype)


def norm_kernel(core_ref, parts_ref, gain_ref, kv_ref, raw_ref):
    total = parts_ref[0].astype(f32)
    for i in range(1, parts_ref.shape[0]):
        total = total + parts_ref[i].astype(f32)
    keys, _ = head_norm(total, gain_ref[...])
    raw_ref[...] = total
    kv_ref[...] = by_core(core_ref[0], keys, total).astype(bf16)


def query_kernel(query_ref, gain_ref, normed_ref):
    head = gain_ref.shape[1]
    for low in range(0, query_ref.shape[1], head):
        cols = slice(low, low + head)
        normed, _ = head_norm(query_ref[:, cols].astype(f32), gain_ref[...])
        normed_ref[:, cols] = normed.astype(bf16)


def attention_kernel(
    core_ref, mine_ref, other_ref, normed_ref, up_ref, seen_ref,
    probs_ref, score_grad_ref, send_ref, keep_ref,
):
    core = core_ref[0]
    rows, head = mine_ref.shape
    text, width = normed_ref.shape
    scale = head ** (-0.5)
    keys = by_core(core, mine_ref[...], other_ref[...])
    values = by_core(core, other_ref[...], mine_ref[...])
    seen = seen_ref[...]
    empty = jnp.where(seen == 0, 1.0, 0.0)
    visible = jnp.concatenate(
        [jnp.broadcast_to(i < seen, (TILE_ROWS, text)) for i in range(rows // TILE_ROWS)], 0
    )
    key_grad = jnp.zeros((rows, head), f32)
    value_grad = jnp.zeros((rows, head), f32)
    for h in range(width // head):
        cols = slice(h * head, (h + 1) * head)
        up = up_ref[:, cols]
        normed = normed_ref[:, cols]
        scores = dot(keys, normed, BOTH_LAST)
        expo = jnp.where(visible, jnp.exp2(scores * (scale * LOG2_E)), 0.0)
        totals = jnp.sum(expo, 0, keepdims=True) + empty
        probs = expo * (1.0 / totals)
        probs_low = probs.astype(bf16)
        prob_grad = dot(values, up, BOTH_LAST)
        row_dot = jnp.sum(probs * prob_grad, 0, keepdims=True)
        score_grad = (probs * (prob_grad - row_dot)).astype(bf16)
        key_grad = key_grad + dot(score_grad, normed)
        value_grad = value_grad + dot(probs_low, up)
        probs_ref[h] = probs_low
        score_grad_ref[h] = score_grad
    key_grad = key_grad * scale
    keep_ref[...] = by_core(core, key_grad, value_grad)
    send_ref[...] = by_core(core, value_grad, key_grad).astype(bf16)


def send_heads(held, out_ref, sems, width, fill):
    copies = []
    for h in range(held.shape[1] // width):
        cols = slice(h * width, (h + 1) * width)
        held[:, cols] = fill(h, cols).astype(bf16)
        copies.append(pltpu.make_async_copy(held.at[:, cols], out_ref.at[:, cols], sems.at[h]))
        copies[-1].start()
    for copy in copies:
        copy.wait()


def context_kernel(core_ref, mine_ref, other_ref, probs_ref, context_ref, held, sems):
    values = by_core(core_ref[0], other_ref[...], mine_ref[...])
    values_t = values.astype(f32).T.astype(bf16)
    send_heads(
        held, context_ref, sems, values.shape[1], lambda h, _: dot(values_t, probs_ref[h]).T
    )


def normed_grad_kernel(core_ref, mine_ref, other_ref, score_grad_ref, out_ref):
    keys = by_core(core_ref[0], mine_ref[...], other_ref[...])
    keys_t = keys.astype(f32).T.astype(bf16)
    for h in range(score_grad_ref.shape[0]):
        out_ref[h] = (dot(keys_t, score_grad_ref[h]) * keys.shape[1] ** (-0.5)).astype(bf16)


def query_grad_kernel(
    query_ref, gain_ref, normed_grad_ref, query_grad_ref, held, sems, query_held, query_sem
):
    copy = pltpu.make_async_copy(query_ref, query_held, query_sem)
    copy.start()
    gain = gain_ref[...]
    copy.wait()

    def fill(h, cols):
        query = query_held[:, cols].astype(f32)
        _, inverse = head_norm(query, gain)
        return head_norm_back(query, inverse, gain, normed_grad_ref[h].astype(f32).T)

    send_heads(held, query_grad_ref, sems, gain.shape[1], fill)


def kv_grad_kernel(core_ref, keep_ref, received_ref, raw_ref, gain_ref, out_ref):
    total = keep_ref[...] + received_ref[...].astype(f32)
    gain = gain_ref[...]
    raw = raw_ref[...]
    _, inverse = head_norm(raw, gain)
    key_raw_grad = head_norm_back(raw, inverse, gain, total)
    kv_grad = by_core(core_ref[0], key_raw_grad, total).astype(bf16)
    for i in range(out_ref.shape[0]):
        out_ref[i] = kv_grad


def image_product(grads_ref, weight_ref, now):
    kv_heads, _, head = grads_ref.shape
    total = None
    for low in range(0, kv_heads, 2):
        pair = jnp.concatenate([grads_ref[low], grads_ref[low + 1]], 1)
        term = dot(pair, weight_ref[now, low * head : (low + 2) * head], BOTH_LAST)
        total = term if total is None else total + term
    return total


def image_kernel(core_ref, grads_ref, key_ref, value_ref, out_ref):
    for kind, weight_ref in enumerate((key_ref, value_ref)):

        @pl.when(core_ref[0] == kind)
        def _(weight_ref=weight_ref):
            out_ref[...] = image_product(grads_ref, weight_ref, slice(None)).astype(out_ref.dtype)


def add_kernel(own_ref, received_ref, out_ref, held, sems):
    copies = []
    step = held.shape[0] // ADD_STEPS
    for i in range(ADD_STEPS):
        now = slice(i * step, (i + 1) * step)
        held[now] = (own_ref[now] + received_ref[now].astype(f32)).astype(bf16)
        copies.append(pltpu.make_async_copy(held.at[now], out_ref.at[now], sems.at[i]))
        copies[-1].start()
    for copy in copies:
        copy.wait()


def weight_grad_kernel(
    core_ref, rows_ref, mine_ref, other_ref, key_ref, value_ref, other_held, sems
):
    kv_heads, _, head = mine_ref.shape
    copies = [
        pltpu.make_async_copy(other_ref.at[h], other_held.at[h], sems.at[h])
        for h in range(kv_heads)
    ]
    for copy in copies:
        copy.start()
    core = core_ref[0]
    rows_t = rows_ref[...].astype(f32).T.astype(bf16)
    for low in range(0, kv_heads, 2):
        cols = slice(low * head, (low + 2) * head)
        mine = jnp.concatenate([mine_ref[low], mine_ref[low + 1]], 1)
        copies[low].wait()
        copies[low + 1].wait()
        other = jnp.concatenate([other_held[low], other_held[low + 1]], 1)
        key_ref[:, cols] = dot(rows_t, by_core(core, mine, other)).astype(bf16)
        value_ref[:, cols] = dot(rows_t, by_core(core, other, mine)).astype(bf16)


def sum_kernel(parts_ref, out_ref):
    total = parts_ref[0].astype(f32)
    for i in range(1, parts_ref.shape[0]):
        total = total + parts_ref[i].astype(f32)
    out_ref[...] = total


def call(kernel, outs, *args, scalar=False, cost=None, scratch=(), to_hbm=(), from_hbm=()):
    many = len(outs) > 1
    shapes = tuple(jax.ShapeDtypeStruct(shape, kind) for shape, kind in outs)
    places = tuple(ANY if i in to_hbm else VMEM for i in range(len(outs)))
    takes = [HBM if i in from_hbm else VMEM for i in range(len(args))]
    if scalar:
        takes[0] = SMEM
    return pl.pallas_call(
        kernel,
        out_shape=shapes if many else shapes[0],
        in_specs=takes,
        out_specs=places if many else places[0],
        scratch_shapes=list(scratch),
        compiler_params=PARAMS,
        cost_estimate=cost,
    )(*args)


def fence(*arrays):
    return lax.optimization_barrier(arrays)


def shards(
    image_rows, queries, key_weight, value_weight, query_gain, key_gain, tiles_seen, context_grad
):
    sections = lax.axis_size("section")
    tp = lax.axis_size("tp")
    chips = tp // CORES
    core = (lax.axis_index("tp") % CORES).astype(jnp.int32).reshape(1)
    same_core = [[i for i in range(tp) if i % CORES == c] for c in range(CORES)]
    swap = [(i, i ^ 1) for i in range(tp)]

    def other_core(x):
        return lax.ppermute(x, "tp", swap)

    def over_chips(x):
        return lax.all_to_all(x, "tp", 0, 0, axis_index_groups=same_core)

    own_rows, features = image_rows.shape
    rows_total = sections * own_rows
    kv_width = key_weight.shape[2]
    head = query_gain.shape[1]
    kv_heads = kv_width // head
    text, width = queries.shape[1:]
    pieces = (kv_heads, rows_total, head)
    square = (rows_total, head)

    key_other = other_core(key_weight[0])
    value_other = other_core(value_weight[0])
    image_rows, core = fence(image_rows, core)
    copies = call(
        copies_kernel, [((sections, own_rows, features), bf16)], image_rows,
        cost=pl.CostEstimate(flops=2**34, bytes_accessed=2**25, transcendentals=0),
    )
    blocks = lax.all_to_all(copies, "section", 0, 0)
    blocks, key_weight, value_weight, key_other, value_other, queries, context_grad = fence(
        blocks, key_weight[0], value_weight[0], key_other, value_other, queries[0], context_grad[0]
    )
    rows = blocks.reshape(rows_total, features)
    rows_other = other_core(rows)
    partial = call(
        project_kernel, [(pieces, f32)], core, rows, key_weight, value_weight, scalar=True
    )
    partial = call(
        project_kernel, [(pieces, bf16)],
        core, rows_other, key_other, value_other, partial, scalar=True,
    )
    parts = over_chips(partial)
    kv_mine, raw = call(
        norm_kernel, [(square, bf16), (square, f32)], core, parts, key_gain, scalar=True
    )
    kv_mine, raw, queries, context_grad = fence(kv_mine, raw, queries, context_grad)
    kv_other = other_core(kv_mine)
    normed = call(
        query_kernel, [((text, width), bf16)], queries, query_gain,
        cost=pl.CostEstimate(flops=2**30, bytes_accessed=2**20, transcendentals=0),
    )
    per_head = (width // head, rows_total, text)
    probs, score_grad, send, keep = call(
        attention_kernel, [(per_head, bf16), (per_head, bf16), (square, bf16), (square, f32)],
        core, kv_mine, kv_other, normed, context_grad, tiles_seen[None], scalar=True,
    )
    send, keep, raw, probs, score_grad = fence(send, keep, raw, probs, score_grad)
    received = other_core(send)
    out_scratch = [
        pltpu.VMEM((text, width), bf16), pltpu.SemaphoreType.DMA((width // head,))
    ]
    context = call(
        context_kernel, [((text, width), bf16)], core, kv_mine, kv_other, probs,
        scalar=True, to_hbm=(0,), scratch=out_scratch,
        cost=pl.CostEstimate(flops=2**30, bytes_accessed=2**20, transcendentals=0),
    )
    received, context = fence(received, context)
    copies = call(
        kv_grad_kernel, [(pieces, bf16)], core, keep, received, raw, key_gain, scalar=True
    )
    grads = over_chips(copies)
    image_send = call(
        image_kernel, [((rows_total, features), bf16)],
        core, grads, key_other, value_other, scalar=True,
    )
    image_send, grads, score_grad = fence(image_send, grads, score_grad)
    received = other_core(image_send)
    image_own = call(
        image_kernel, [((rows_total, features), f32)],
        core, grads, key_weight, value_weight, scalar=True,
    )
    normed_grad = call(
        normed_grad_kernel, [((width // head, head, text), bf16)],
        core, kv_mine, kv_other, score_grad, scalar=True,
        cost=pl.CostEstimate(flops=2**30, bytes_accessed=2**20, transcendentals=0),
    )
    image_own, received, normed_grad = fence(image_own, received, normed_grad)
    image_part = call(
        add_kernel, [((rows_total, features), bf16)], image_own, received, to_hbm=(0,),
        scratch=[pltpu.VMEM((rows_total, features), bf16), pltpu.SemaphoreType.DMA((ADD_STEPS,))],
    )
    image_part, rows, grads, normed_grad = fence(image_part, rows, grads, normed_grad)
    grads_other = other_core(grads)
    image_parts = lax.all_to_all(
        image_part.reshape(sections, own_rows, features), "section", 0, 0
    )
    key_weight_grad, value_weight_grad = call(
        weight_grad_kernel, [((features, kv_width), bf16)] * 2,
        core, rows, grads, grads_other, scalar=True, from_hbm=(3,),
        scratch=[pltpu.VMEM(pieces, bf16), pltpu.SemaphoreType.DMA((kv_heads,))],
        cost=pl.CostEstimate(
            flops=2 * features * 2 * kv_width * rows_total,
            bytes_accessed=4 * features * 2 * kv_width,
            transcendentals=0,
        ),
    )
    query_grad = call(
        query_grad_kernel, [((text, width), bf16)],
        queries, query_gain, normed_grad, to_hbm=(0,), from_hbm=(0,),
        scratch=out_scratch + [pltpu.VMEM((text, width), bf16), pltpu.SemaphoreType.DMA],
        cost=pl.CostEstimate(flops=2**30, bytes_accessed=2**20, transcendentals=0),
    )
    image_parts, key_weight_grad, value_weight_grad, query_grad = fence(
        image_parts, key_weight_grad, value_weight_grad, query_grad
    )
    image_grad = call(sum_kernel, [((own_rows, features), f32)], image_parts)
    return (
        context[None], query_grad[None], key_weight_grad[None], value_weight_grad[None], image_grad
    )


def solution(mesh):
    return jax.shard_map(
        shards,
        mesh=mesh,
        in_specs=(
            P("section", "tp"),
            P("section", None, "tp"),
            P("section", "tp", None),
            P("section", "tp", None),
            P("section", None),
            P("section", None),
            P(),
            P("section", None, "tp"),
        ),
        out_specs=(
            P("section", None, "tp"),
            P("section", None, "tp"),
            P("section", "tp", None),
            P("section", "tp", None),
            P("section", "tp"),
        ),
        check_vma=False,
    )
```

```python
import jax
import jax.numpy as jnp
from jax import lax
from jax.experimental import pallas as pl
from jax.experimental.pallas import tpu as pltpu
from jax.sharding import PartitionSpec as P

TILE_ROWS = 96
CORES = 2
SIDE = 4
LOG2_E = 1.4426950408889634
epsilon = 1e-05

f32 = jnp.float32
bf16 = jnp.bfloat16

BOTH_LAST = (((1,), (1,)), ((), ()))

ANY = pl.BlockSpec(memory_space=pl.ANY)
VMEM = pl.BlockSpec(memory_space=pltpu.VMEM)
SMEM = pl.BlockSpec(memory_space=pltpu.SMEM)
PARAMS = pltpu.CompilerParams(vmem_limit_bytes=16 * 1024 * 1024)


def dot(a, b, dims=(((1,), (0,)), ((), ()))):
    return lax.dot_general(a, b, dims, preferred_element_type=f32)


def head_norm(raw_rows, gain_row):
    inverse = lax.rsqrt(jnp.mean(raw_rows * raw_rows, -1, keepdims=True) + epsilon)
    return (raw_rows * inverse * gain_row, inverse)


def head_norm_back(raw_rows, inverse, gain_row, upstream):
    scaled = upstream * gain_row
    return inverse * scaled - raw_rows * (
        inverse * inverse * inverse * jnp.mean(raw_rows * scaled, -1, keepdims=True)
    )


def wrap(i):
    return lax.rem(i + SIDE, SIDE)


def by_core(core, zero, one):
    return jnp.where(core == 0, zero, one)


def copy_kernel(rows_ref, out_ref):
    out_ref[...] = rows_ref[...]


def gather_z_kernel(z_ref, *refs):
    *blocks, out_ref = refs
    for k, block in enumerate(blocks):
        out_ref[wrap(z_ref[0] - k)] = block[...]


def gather_y_kernel(y_ref, *refs):
    *blocks, out_ref = refs
    for k, block in enumerate(blocks):
        y = wrap(y_ref[0] - k)
        for z in range(SIDE):
            out_ref[y * SIDE + z] = block[z]


def project_kernel(core_ref, rows_ref, key_ref, value_ref, *refs):
    *before, out_ref = refs
    kv_heads, _, head = out_ref.shape
    rows = rows_ref[...]
    for kind, weight_ref in enumerate((key_ref, value_ref)):

        @pl.when(core_ref[0] == kind)
        def _(weight_ref=weight_ref):
            for low in range(0, kv_heads, 2):
                pair = dot(rows, weight_ref[:, low * head : (low + 2) * head])
                for i in range(2):
                    here = pair[:, i * head : (i + 1) * head]
                    if before:
                        here = here + before[0][low + i]
                    out_ref[low + i] = here.astype(out_ref.dtype)


def norm_kernel(core_ref, parts_ref, gain_ref, kv_ref, raw_ref):
    total = parts_ref[0].astype(f32)
    for i in range(1, parts_ref.shape[0]):
        total = total + parts_ref[i].astype(f32)
    keys, _ = head_norm(total, gain_ref[...])
    raw_ref[...] = total
    kv_ref[...] = by_core(core_ref[0], keys, total).astype(bf16)


def query_kernel(query_ref, gain_ref, normed_ref):
    head = gain_ref.shape[1]
    for low in range(0, query_ref.shape[1], head):
        cols = slice(low, low + head)
        normed, _ = head_norm(query_ref[:, cols].astype(f32), gain_ref[...])
        normed_ref[:, cols] = normed.astype(bf16)


def attention_kernel(
    core_ref, mine_ref, other_ref, normed_ref, up_ref, seen_ref,
    probs_ref, score_grad_ref, send_ref, keep_ref,
):
    core = core_ref[0]
    rows, head = mine_ref.shape
    text, width = normed_ref.shape
    scale = head ** (-0.5)
    keys = by_core(core, mine_ref[...], other_ref[...])
    values = by_core(core, other_ref[...], mine_ref[...])
    seen = seen_ref[...]
    empty = jnp.where(seen == 0, 1.0, 0.0)
    visible = jnp.concatenate(
        [jnp.broadcast_to(i < seen, (TILE_ROWS, text)) for i in range(rows // TILE_ROWS)], 0
    )
    key_grad = jnp.zeros((rows, head), f32)
    value_grad = jnp.zeros((rows, head), f32)
    for h in range(width // head):
        cols = slice(h * head, (h + 1) * head)
        up = up_ref[:, cols]
        normed = normed_ref[:, cols]
        scores = dot(keys, normed, BOTH_LAST)
        expo = jnp.where(visible, jnp.exp2(scores * (scale * LOG2_E)), 0.0)
        totals = jnp.sum(expo, 0, keepdims=True) + empty
        probs = expo * (1.0 / totals)
        probs_low = probs.astype(bf16)
        prob_grad = dot(values, up, BOTH_LAST)
        row_dot = jnp.sum(probs * prob_grad, 0, keepdims=True)
        score_grad = (probs * (prob_grad - row_dot)).astype(bf16)
        key_grad = key_grad + dot(score_grad, normed)
        value_grad = value_grad + dot(probs_low, up)
        probs_ref[h] = probs_low
        score_grad_ref[h] = score_grad
    key_grad = key_grad * scale
    keep_ref[...] = by_core(core, key_grad, value_grad)
    send_ref[...] = by_core(core, value_grad, key_grad).astype(bf16)


def send_heads(held, out_ref, sems, width, fill):
    copies = []
    for h in range(held.shape[1] // width):
        cols = slice(h * width, (h + 1) * width)
        held[:, cols] = fill(h, cols).astype(bf16)
        copies.append(pltpu.make_async_copy(held.at[:, cols], out_ref.at[:, cols], sems.at[h]))
        copies[-1].start()
    for copy in copies:
        copy.wait()


def context_kernel(core_ref, mine_ref, other_ref, probs_ref, context_ref, held, sems):
    values = by_core(core_ref[0], other_ref[...], mine_ref[...])
    values_t = values.astype(f32).T.astype(bf16)
    send_heads(
        held, context_ref, sems, values.shape[1], lambda h, _: dot(values_t, probs_ref[h]).T
    )


def query_grad_kernel(
    core_ref, mine_ref, other_ref, query_ref, gain_ref, score_grad_ref, query_grad_ref, held, sems
):
    keys = by_core(core_ref[0], mine_ref[...], other_ref[...])
    keys_t = keys.astype(f32).T.astype(bf16)
    head = keys.shape[1]
    gain = gain_ref[...]

    def fill(h, cols):
        query = query_ref[:, cols].astype(f32)
        _, inverse = head_norm(query, gain)
        normed_grad = dot(keys_t, score_grad_ref[h]).T * head ** (-0.5)
        return head_norm_back(query, inverse, gain, normed_grad)

    send_heads(held, query_grad_ref, sems, head, fill)


def kv_grad_kernel(core_ref, keep_ref, received_ref, raw_ref, gain_ref, out_ref):
    total = keep_ref[...] + received_ref[...].astype(f32)
    gain = gain_ref[...]
    raw = raw_ref[...]
    _, inverse = head_norm(raw, gain)
    key_raw_grad = head_norm_back(raw, inverse, gain, total)
    kv_grad = by_core(core_ref[0], key_raw_grad, total).astype(bf16)
    for i in range(out_ref.shape[0]):
        out_ref[i] = kv_grad


def image_product(grads_ref, weight_ref, now):
    kv_heads, _, head = grads_ref.shape
    total = None
    for low in range(0, kv_heads, 2):
        pair = jnp.concatenate([grads_ref[low], grads_ref[low + 1]], 1)
        term = dot(pair, weight_ref[now, low * head : (low + 2) * head], BOTH_LAST)
        total = term if total is None else total + term
    return total


def image_kernel(core_ref, grads_ref, key_ref, value_ref, out_ref):
    for kind, weight_ref in enumerate((key_ref, value_ref)):

        @pl.when(core_ref[0] == kind)
        def _(weight_ref=weight_ref):
            out_ref[...] = image_product(grads_ref, weight_ref, slice(None)).astype(out_ref.dtype)


def scatter_y_kernel(y_ref, own_ref, received_ref, keep_ref, *send_refs):
    for k, out_ref in enumerate((keep_ref, *send_refs)):
        y = wrap(y_ref[0] + k)
        for z in range(SIDE):
            i = y * SIDE + z
            out_ref[z] = (own_ref[i] + received_ref[i].astype(f32)).astype(out_ref.dtype)


def scatter_z_kernel(z_ref, keep_ref, *refs):
    received, outs, total_ref = refs[: SIDE - 1], refs[SIDE - 1 : -1], refs[-1]
    for z in range(SIDE):
        total = keep_ref[z]
        for block in received:
            total = total + block[z].astype(f32)
        total_ref[z] = total
    for k, out_ref in enumerate(outs):
        out_ref[...] = total_ref[wrap(z_ref[0] + k)].astype(out_ref.dtype)


def sum_kernel(keep_ref, *refs):
    *received, out_ref = refs
    total = keep_ref[...]
    for block in received:
        total = total + block[...].astype(f32)
    out_ref[...] = total


def weight_grad_kernel(core_ref, rows_ref, mine_ref, other_ref, key_ref, value_ref):
    kv_heads, _, head = mine_ref.shape
    core = core_ref[0]
    rows_t = rows_ref[...].astype(f32).T.astype(bf16)
    for low in range(0, kv_heads, 2):
        cols = slice(low * head, (low + 2) * head)
        mine = jnp.concatenate([mine_ref[low], mine_ref[low + 1]], 1)
        other = jnp.concatenate([other_ref[low], other_ref[low + 1]], 1)
        key_ref[:, cols] = dot(rows_t, by_core(core, mine, other)).astype(bf16)
        value_ref[:, cols] = dot(rows_t, by_core(core, other, mine)).astype(bf16)


def call(kernel, outs, *args, scalar=False, cost=None, scratch=(), to_hbm=()):
    many = len(outs) > 1
    shapes = tuple(jax.ShapeDtypeStruct(shape, kind) for shape, kind in outs)
    places = tuple(ANY if i in to_hbm else VMEM for i in range(len(outs)))
    takes = [VMEM] * len(args)
    if scalar:
        takes[0] = SMEM
    return pl.pallas_call(
        kernel,
        out_shape=shapes if many else shapes[0],
        in_specs=takes,
        out_specs=places if many else places[0],
        scratch_shapes=list(scratch),
        compiler_params=PARAMS,
        cost_estimate=cost,
    )(*args)


def fence(*arrays):
    return lax.optimization_barrier(arrays)


def shards(
    image_rows, queries, key_weight, value_weight, query_gain, key_gain, tiles_seen, context_grad
):
    sections = lax.axis_size("section")
    tp = lax.axis_size("tp")
    chips = tp // CORES
    core = (lax.axis_index("tp") % CORES).astype(jnp.int32).reshape(1)
    same_core = [[i for i in range(tp) if i % CORES == c] for c in range(CORES)]
    swap = [(i, i ^ 1) for i in range(tp)]

    def other_core(x):
        return lax.ppermute(x, "tp", swap)

    def over_chips(x):
        return lax.all_to_all(x, "tp", 0, 0, axis_index_groups=same_core)

    own_rows, features = image_rows.shape
    rows_total = sections * own_rows
    kv_width = key_weight.shape[2]
    head = query_gain.shape[1]
    kv_heads = kv_width // head
    text, width = queries.shape[1:]
    pieces = (kv_heads, rows_total, head)
    square = (rows_total, head)

    key_other = other_core(key_weight[0])
    value_other = other_core(value_weight[0])
    block = (own_rows, features)
    column = (SIDE, *block)
    section = lax.axis_index("section").astype(jnp.int32)
    my_y, my_z = (section // SIDE).reshape(1), (section % SIDE).reshape(1)

    def along_z(x, k):
        to = [(i, i // SIDE * SIDE + (i + k) % SIDE) for i in range(sections)]
        return lax.ppermute(x, "section", to)

    def along_y(x, k):
        return lax.ppermute(x, "section", [(i, (i + k * SIDE) % sections) for i in range(sections)])

    image_rows, core, my_y, my_z = fence(image_rows, core, my_y, my_z)
    others = [along_z(image_rows, k) for k in range(1, SIDE)]
    own = call(
        copy_kernel, [(block, bf16)], image_rows,
        cost=pl.CostEstimate(flops=2**30, bytes_accessed=2**20, transcendentals=0),
    )
    rows_z = call(
        gather_z_kernel, [(column, bf16)], my_z, own, *others, scalar=True,
        cost=pl.CostEstimate(flops=2**34, bytes_accessed=2**25, transcendentals=0),
    )
    others = [along_y(rows_z, k) for k in range(1, SIDE)]
    blocks = call(
        gather_y_kernel, [((sections, *block), bf16)], my_y, rows_z, *others, scalar=True
    )
    blocks, key_weight, value_weight, key_other, value_other, queries, context_grad = fence(
        blocks, key_weight[0], value_weight[0], key_other, value_other, queries[0], context_grad[0]
    )
    rows = blocks.reshape(rows_total, features)
    rows_other = other_core(rows)
    partial = call(
        project_kernel, [(pieces, f32)], core, rows, key_weight, value_weight, scalar=True
    )
    partial = call(
        project_kernel, [(pieces, bf16)],
        core, rows_other, key_other, value_other, partial, scalar=True,
    )
    parts = over_chips(partial)
    kv_mine, raw = call(
        norm_kernel, [(square, bf16), (square, f32)], core, parts, key_gain, scalar=True
    )
    kv_mine, raw, queries, context_grad = fence(kv_mine, raw, queries, context_grad)
    kv_other = other_core(kv_mine)
    normed = call(
        query_kernel, [((text, width), bf16)], queries, query_gain,
        cost=pl.CostEstimate(flops=2**30, bytes_accessed=2**20, transcendentals=0),
    )
    per_head = (width // head, rows_total, text)
    probs, score_grad, send, keep = call(
        attention_kernel, [(per_head, bf16), (per_head, bf16), (square, bf16), (square, f32)],
        core, kv_mine, kv_other, normed, context_grad, tiles_seen[None], scalar=True,
    )
    send, keep, raw, probs, score_grad = fence(send, keep, raw, probs, score_grad)
    received = other_core(send)
    out_scratch = [
        pltpu.VMEM((text, width), bf16), pltpu.SemaphoreType.DMA((width // head,))
    ]
    context = call(
        context_kernel, [((text, width), bf16)], core, kv_mine, kv_other, probs,
        scalar=True, to_hbm=(0,), scratch=out_scratch,
        cost=pl.CostEstimate(flops=2**30, bytes_accessed=2**20, transcendentals=0),
    )
    received, context = fence(received, context)
    copies = call(
        kv_grad_kernel, [(pieces, bf16)], core, keep, received, raw, key_gain, scalar=True
    )
    grads = over_chips(copies)
    image_send = call(
        image_kernel, [((rows_total, features), bf16)],
        core, grads, key_other, value_other, scalar=True,
    )
    image_send, grads, score_grad = fence(image_send, grads, score_grad)
    received = other_core(image_send)
    image_own = call(
        image_kernel, [((rows_total, features), f32)],
        core, grads, key_weight, value_weight, scalar=True,
    )
    image_own, received = fence(image_own, received)
    keep, *sends = call(
        scatter_y_kernel, [(column, f32)] + [(column, bf16)] * (SIDE - 1),
        my_y, image_own.reshape(sections, *block), received.reshape(sections, *block),
        scalar=True,
    )
    keep, sends, rows, grads, score_grad = fence(keep, sends, rows, grads, score_grad)
    received = [along_y(x, k + 1) for k, x in enumerate(sends)]
    grads_other = other_core(grads)
    key_weight_grad, value_weight_grad = call(
        weight_grad_kernel, [((features, kv_width), bf16)] * 2,
        core, rows, grads, grads_other, scalar=True,
        cost=pl.CostEstimate(
            flops=2 * features * 2 * kv_width * rows_total,
            bytes_accessed=4 * features * 2 * kv_width,
            transcendentals=0,
        ),
    )
    received, key_weight_grad, value_weight_grad, score_grad = fence(
        received, key_weight_grad, value_weight_grad, score_grad
    )
    keep, *sends = call(
        scatter_z_kernel, [(block, f32)] + [(block, bf16)] * (SIDE - 1),
        my_z, keep, *received, scalar=True, scratch=[pltpu.VMEM(column, f32)],
    )
    keep, sends, score_grad = fence(keep, sends, score_grad)
    received = [along_z(x, k + 1) for k, x in enumerate(sends)]
    query_grad = call(
        query_grad_kernel, [((text, width), bf16)],
        core, kv_mine, kv_other, queries, query_gain, score_grad,
        scalar=True, to_hbm=(0,), scratch=out_scratch,
        cost=pl.CostEstimate(flops=2**30, bytes_accessed=2**20, transcendentals=0),
    )
    received, query_grad = fence(received, query_grad)
    image_grad = call(sum_kernel, [(block, f32)], keep, *received)
    return (
        context[None], query_grad[None], key_weight_grad[None], value_weight_grad[None], image_grad
    )


def solution(mesh):
    return jax.shard_map(
        shards,
        mesh=mesh,
        in_specs=(
            P("section", "tp"),
            P("section", None, "tp"),
            P("section", "tp", None),
            P("section", "tp", None),
            P("section", None),
            P("section", None),
            P(),
            P("section", None, "tp"),
        ),
        out_specs=(
            P("section", None, "tp"),
            P("section", None, "tp"),
            P("section", "tp", None),
            P("section", "tp", None),
            P("section", "tp"),
        ),
        check_vma=False,
    )
```

```python
import jax
import jax.numpy as jnp
from jax import lax
from jax.experimental import pallas as pl
from jax.experimental.pallas import tpu as pltpu
from jax.sharding import PartitionSpec as P

TILE_ROWS = 96
CORES = 2
SIDE = 4
STEPS = (0, 1, 3, 2)
LATE_STEPS = (0, 2, 1, 3)
LOG2_E = 1.4426950408889634
epsilon = 1e-05

f32 = jnp.float32
bf16 = jnp.bfloat16

BOTH_LAST = (((1,), (1,)), ((), ()))

ANY = pl.BlockSpec(memory_space=pl.ANY)
VMEM = pl.BlockSpec(memory_space=pltpu.VMEM)
SMEM = pl.BlockSpec(memory_space=pltpu.SMEM)
PARAMS = pltpu.CompilerParams(vmem_limit_bytes=16 * 1024 * 1024)


def dot(a, b, dims=(((1,), (0,)), ((), ()))):
    return lax.dot_general(a, b, dims, preferred_element_type=f32)


def head_norm(raw_rows, gain_row):
    inverse = lax.rsqrt(jnp.mean(raw_rows * raw_rows, -1, keepdims=True) + epsilon)
    return (raw_rows * inverse * gain_row, inverse)


def head_norm_back(raw_rows, inverse, gain_row, upstream):
    scaled = upstream * gain_row
    return inverse * scaled - raw_rows * (
        inverse * inverse * inverse * jnp.mean(raw_rows * scaled, -1, keepdims=True)
    )


def wrap(i):
    return lax.rem(i + SIDE, SIDE)


def by_core(core, zero, one):
    return jnp.where(core == 0, zero, one)


def copy_kernel(rows_ref, out_ref):
    out_ref[...] = rows_ref[...]


def gather_z_kernel(z_ref, *refs):
    *blocks, out_ref = refs
    for k, block in zip(STEPS, blocks):
        out_ref[wrap(z_ref[0] - k)] = block[...]


def gather_y_kernel(y_ref, *refs):
    *blocks, out_ref = refs
    for k, block in zip(STEPS, blocks):
        y = wrap(y_ref[0] - k)
        for z in range(SIDE):
            out_ref[y * SIDE + z] = block[z]


def project_kernel(core_ref, rows_ref, key_ref, value_ref, *refs):
    *before, out_ref = refs
    kv_heads, _, head = out_ref.shape
    rows = rows_ref[...]
    for kind, weight_ref in enumerate((key_ref, value_ref)):

        @pl.when(core_ref[0] == kind)
        def _(weight_ref=weight_ref):
            for low in range(0, kv_heads, 2):
                pair = dot(rows, weight_ref[:, low * head : (low + 2) * head])
                for i in range(2):
                    here = pair[:, i * head : (i + 1) * head]
                    if before:
                        here = here + before[0][low + i]
                    out_ref[low + i] = here.astype(out_ref.dtype)


def norm_kernel(core_ref, parts_ref, gain_ref, kv_ref, raw_ref):
    total = parts_ref[0].astype(f32)
    for i in range(1, parts_ref.shape[0]):
        total = total + parts_ref[i].astype(f32)
    keys, _ = head_norm(total, gain_ref[...])
    raw_ref[...] = total
    kv_ref[...] = by_core(core_ref[0], keys, total).astype(bf16)


def query_kernel(query_ref, gain_ref, normed_ref):
    head = gain_ref.shape[1]
    for low in range(0, query_ref.shape[1], head):
        cols = slice(low, low + head)
        normed, _ = head_norm(query_ref[:, cols].astype(f32), gain_ref[...])
        normed_ref[:, cols] = normed.astype(bf16)


def attention_kernel(
    core_ref, mine_ref, other_ref, normed_ref, up_ref, seen_ref,
    probs_ref, score_grad_ref, send_ref, keep_ref,
):
    core = core_ref[0]
    rows, head = mine_ref.shape
    text, width = normed_ref.shape
    scale = head ** (-0.5)
    keys = by_core(core, mine_ref[...], other_ref[...])
    values = by_core(core, other_ref[...], mine_ref[...])
    seen = seen_ref[...]
    empty = jnp.where(seen == 0, 1.0, 0.0)
    visible = jnp.concatenate(
        [jnp.broadcast_to(i < seen, (TILE_ROWS, text)) for i in range(rows // TILE_ROWS)], 0
    )
    key_grad = jnp.zeros((rows, head), f32)
    value_grad = jnp.zeros((rows, head), f32)
    for h in range(width // head):
        cols = slice(h * head, (h + 1) * head)
        up = up_ref[:, cols]
        normed = normed_ref[:, cols]
        scores = dot(keys, normed, BOTH_LAST)
        expo = jnp.where(visible, jnp.exp2(scores * (scale * LOG2_E)), 0.0)
        totals = jnp.sum(expo, 0, keepdims=True) + empty
        probs = expo * (1.0 / totals)
        probs_low = probs.astype(bf16)
        prob_grad = dot(values, up, BOTH_LAST)
        row_dot = jnp.sum(probs * prob_grad, 0, keepdims=True)
        score_grad = (probs * (prob_grad - row_dot)).astype(bf16)
        key_grad = key_grad + dot(score_grad, normed)
        value_grad = value_grad + dot(probs_low, up)
        probs_ref[h] = probs_low
        score_grad_ref[h] = score_grad
    key_grad = key_grad * scale
    keep_ref[...] = by_core(core, key_grad, value_grad)
    send_ref[...] = by_core(core, value_grad, key_grad).astype(bf16)


def send_heads(held, out_ref, sems, width, fill):
    copies = []
    for h in range(held.shape[1] // width):
        cols = slice(h * width, (h + 1) * width)
        held[:, cols] = fill(h, cols).astype(bf16)
        copies.append(pltpu.make_async_copy(held.at[:, cols], out_ref.at[:, cols], sems.at[h]))
        copies[-1].start()
    for copy in copies:
        copy.wait()


def context_kernel(core_ref, mine_ref, other_ref, probs_ref, context_ref, held, sems):
    values = by_core(core_ref[0], other_ref[...], mine_ref[...])
    values_t = values.astype(f32).T.astype(bf16)
    send_heads(
        held, context_ref, sems, values.shape[1], lambda h, _: dot(values_t, probs_ref[h]).T
    )


def query_grad_kernel(
    core_ref, mine_ref, other_ref, query_ref, gain_ref, score_grad_ref, query_grad_ref, held, sems
):
    keys = by_core(core_ref[0], mine_ref[...], other_ref[...])
    keys_t = keys.astype(f32).T.astype(bf16)
    head = keys.shape[1]
    gain = gain_ref[...]

    def fill(h, cols):
        query = query_ref[:, cols].astype(f32)
        _, inverse = head_norm(query, gain)
        normed_grad = dot(keys_t, score_grad_ref[h]).T * head ** (-0.5)
        return head_norm_back(query, inverse, gain, normed_grad)

    send_heads(held, query_grad_ref, sems, head, fill)


def kv_grad_kernel(core_ref, keep_ref, received_ref, raw_ref, gain_ref, out_ref):
    total = keep_ref[...] + received_ref[...].astype(f32)
    gain = gain_ref[...]
    raw = raw_ref[...]
    _, inverse = head_norm(raw, gain)
    key_raw_grad = head_norm_back(raw, inverse, gain, total)
    kv_grad = by_core(core_ref[0], key_raw_grad, total).astype(bf16)
    for i in range(out_ref.shape[0]):
        out_ref[i] = kv_grad


def image_product(grads_ref, weight_ref, now):
    kv_heads, _, head = grads_ref.shape
    total = None
    for low in range(0, kv_heads, 2):
        pair = jnp.concatenate([grads_ref[low], grads_ref[low + 1]], 1)
        term = dot(pair, weight_ref[now, low * head : (low + 2) * head], BOTH_LAST)
        total = term if total is None else total + term
    return total


def image_kernel(core_ref, grads_ref, key_ref, value_ref, out_ref):
    for kind, weight_ref in enumerate((key_ref, value_ref)):

        @pl.when(core_ref[0] == kind)
        def _(weight_ref=weight_ref):
            out_ref[...] = image_product(grads_ref, weight_ref, slice(None)).astype(out_ref.dtype)


def scatter_y_kernel(y_ref, own_ref, received_ref, keep_ref, *send_refs):
    for k, out_ref in zip(LATE_STEPS, (keep_ref, *send_refs)):
        y = wrap(y_ref[0] + k)
        for z in range(SIDE):
            i = y * SIDE + z
            out_ref[z] = (own_ref[i] + received_ref[i].astype(f32)).astype(out_ref.dtype)


def scatter_z_kernel(z_ref, keep_ref, *refs):
    received, outs, total_ref = refs[: SIDE - 1], refs[SIDE - 1 : -1], refs[-1]
    for z in range(SIDE):
        total = keep_ref[z]
        for block in received:
            total = total + block[z].astype(f32)
        total_ref[z] = total
    for k, out_ref in zip(LATE_STEPS, outs):
        out_ref[...] = total_ref[wrap(z_ref[0] + k)].astype(out_ref.dtype)


def sum_kernel(keep_ref, *refs):
    *received, out_ref = refs
    total = keep_ref[...]
    for block in received:
        total = total + block[...].astype(f32)
    out_ref[...] = total


def weight_grad_kernel(core_ref, rows_ref, mine_ref, other_ref, key_ref, value_ref):
    kv_heads, _, head = mine_ref.shape
    core = core_ref[0]
    rows_t = rows_ref[...].astype(f32).T.astype(bf16)
    for low in range(0, kv_heads, 2):
        cols = slice(low * head, (low + 2) * head)
        mine = jnp.concatenate([mine_ref[low], mine_ref[low + 1]], 1)
        other = jnp.concatenate([other_ref[low], other_ref[low + 1]], 1)
        key_ref[:, cols] = dot(rows_t, by_core(core, mine, other)).astype(bf16)
        value_ref[:, cols] = dot(rows_t, by_core(core, other, mine)).astype(bf16)


def call(kernel, outs, *args, scalar=False, cost=None, scratch=(), to_hbm=()):
    many = len(outs) > 1
    shapes = tuple(jax.ShapeDtypeStruct(shape, kind) for shape, kind in outs)
    places = tuple(ANY if i in to_hbm else VMEM for i in range(len(outs)))
    takes = [VMEM] * len(args)
    if scalar:
        takes[0] = SMEM
    return pl.pallas_call(
        kernel,
        out_shape=shapes if many else shapes[0],
        in_specs=takes,
        out_specs=places if many else places[0],
        scratch_shapes=list(scratch),
        compiler_params=PARAMS,
        cost_estimate=cost,
    )(*args)


def fence(*arrays):
    return lax.optimization_barrier(arrays)


def shards(
    image_rows, queries, key_weight, value_weight, query_gain, key_gain, tiles_seen, context_grad
):
    sections = lax.axis_size("section")
    tp = lax.axis_size("tp")
    chips = tp // CORES
    core = (lax.axis_index("tp") % CORES).astype(jnp.int32).reshape(1)
    same_core = [[i for i in range(tp) if i % CORES == c] for c in range(CORES)]
    swap = [(i, i ^ 1) for i in range(tp)]

    def other_core(x):
        return lax.ppermute(x, "tp", swap)

    def over_chips(x):
        return lax.all_to_all(x, "tp", 0, 0, axis_index_groups=same_core)

    own_rows, features = image_rows.shape
    rows_total = sections * own_rows
    kv_width = key_weight.shape[2]
    head = query_gain.shape[1]
    kv_heads = kv_width // head
    text, width = queries.shape[1:]
    pieces = (kv_heads, rows_total, head)
    square = (rows_total, head)

    key_other = other_core(key_weight[0])
    value_other = other_core(value_weight[0])
    block = (own_rows, features)
    column = (SIDE, *block)
    section = lax.axis_index("section").astype(jnp.int32)
    my_y, my_z = (section // SIDE).reshape(1), (section % SIDE).reshape(1)

    def along_z(x, k):
        to = [(i, i // SIDE * SIDE + (i + k) % SIDE) for i in range(sections)]
        return lax.ppermute(x, "section", to)

    def along_y(x, k):
        return lax.ppermute(x, "section", [(i, (i + k * SIDE) % sections) for i in range(sections)])

    image_rows, core, my_y, my_z = fence(image_rows, core, my_y, my_z)
    others = [along_z(image_rows, k) for k in STEPS[1:]]
    own = call(
        copy_kernel, [(block, bf16)], image_rows,
        cost=pl.CostEstimate(flops=2**30, bytes_accessed=2**20, transcendentals=0),
    )
    rows_z = call(
        gather_z_kernel, [(column, bf16)], my_z, own, *others, scalar=True,
        cost=pl.CostEstimate(flops=2**34, bytes_accessed=2**25, transcendentals=0),
    )
    others = [along_y(rows_z, k) for k in STEPS[1:]]
    blocks = call(
        gather_y_kernel, [((sections, *block), bf16)], my_y, rows_z, *others, scalar=True
    )
    blocks, key_weight, value_weight, key_other, value_other, queries, context_grad = fence(
        blocks, key_weight[0], value_weight[0], key_other, value_other, queries[0], context_grad[0]
    )
    rows = blocks.reshape(rows_total, features)
    rows_other = other_core(rows)
    partial = call(
        project_kernel, [(pieces, f32)], core, rows, key_weight, value_weight, scalar=True
    )
    partial = call(
        project_kernel, [(pieces, bf16)],
        core, rows_other, key_other, value_other, partial, scalar=True,
    )
    parts = over_chips(partial)
    kv_mine, raw = call(
        norm_kernel, [(square, bf16), (square, f32)], core, parts, key_gain, scalar=True
    )
    kv_mine, raw, queries, context_grad = fence(kv_mine, raw, queries, context_grad)
    kv_other = other_core(kv_mine)
    normed = call(
        query_kernel, [((text, width), bf16)], queries, query_gain,
        cost=pl.CostEstimate(flops=2**30, bytes_accessed=2**20, transcendentals=0),
    )
    per_head = (width // head, rows_total, text)
    probs, score_grad, send, keep = call(
        attention_kernel, [(per_head, bf16), (per_head, bf16), (square, bf16), (square, f32)],
        core, kv_mine, kv_other, normed, context_grad, tiles_seen[None], scalar=True,
    )
    send, keep, raw, probs, score_grad = fence(send, keep, raw, probs, score_grad)
    received = other_core(send)
    out_scratch = [
        pltpu.VMEM((text, width), bf16), pltpu.SemaphoreType.DMA((width // head,))
    ]
    context = call(
        context_kernel, [((text, width), bf16)], core, kv_mine, kv_other, probs,
        scalar=True, to_hbm=(0,), scratch=out_scratch,
        cost=pl.CostEstimate(flops=2**30, bytes_accessed=2**20, transcendentals=0),
    )
    received, context = fence(received, context)
    copies = call(
        kv_grad_kernel, [(pieces, bf16)], core, keep, received, raw, key_gain, scalar=True
    )
    grads = over_chips(copies)
    image_send = call(
        image_kernel, [((rows_total, features), bf16)],
        core, grads, key_other, value_other, scalar=True,
    )
    image_send, grads, score_grad = fence(image_send, grads, score_grad)
    received = other_core(image_send)
    image_own = call(
        image_kernel, [((rows_total, features), f32)],
        core, grads, key_weight, value_weight, scalar=True,
    )
    image_own, received = fence(image_own, received)
    keep, *sends = call(
        scatter_y_kernel, [(column, f32)] + [(column, bf16)] * (SIDE - 1),
        my_y, image_own.reshape(sections, *block), received.reshape(sections, *block),
        scalar=True,
    )
    keep, sends, rows, grads, score_grad = fence(keep, sends, rows, grads, score_grad)
    received = [along_y(x, k) for k, x in zip(LATE_STEPS[1:], sends)]
    grads_other = other_core(grads)
    key_weight_grad, value_weight_grad = call(
        weight_grad_kernel, [((features, kv_width), bf16)] * 2,
        core, rows, grads, grads_other, scalar=True,
        cost=pl.CostEstimate(
            flops=2 * features * 2 * kv_width * rows_total,
            bytes_accessed=4 * features * 2 * kv_width,
            transcendentals=0,
        ),
    )
    query_grad = call(
        query_grad_kernel, [((text, width), bf16)],
        core, kv_mine, kv_other, queries, query_gain, score_grad,
        scalar=True, to_hbm=(0,), scratch=out_scratch,
        cost=pl.CostEstimate(flops=2**30, bytes_accessed=2**20, transcendentals=0),
    )
    received, key_weight_grad, value_weight_grad, query_grad = fence(
        received, key_weight_grad, value_weight_grad, query_grad
    )
    keep, *sends = call(
        scatter_z_kernel, [(block, f32)] + [(block, bf16)] * (SIDE - 1),
        my_z, keep, *received, scalar=True, scratch=[pltpu.VMEM(column, f32)],
    )
    received = [along_z(x, k) for k, x in zip(LATE_STEPS[1:], sends)]
    image_grad = call(sum_kernel, [(block, f32)], keep, *received)
    return (
        context[None], query_grad[None], key_weight_grad[None], value_weight_grad[None], image_grad
    )


def solution(mesh):
    return jax.shard_map(
        shards,
        mesh=mesh,
        in_specs=(
            P("section", "tp"),
            P("section", None, "tp"),
            P("section", "tp", None),
            P("section", "tp", None),
            P("section", None),
            P("section", None),
            P(),
            P("section", None, "tp"),
        ),
        out_specs=(
            P("section", None, "tp"),
            P("section", None, "tp"),
            P("section", "tp", None),
            P("section", "tp", None),
            P("section", "tp"),
        ),
        check_vma=False,
    )
```

```python
import jax
import jax.numpy as jnp
from jax import lax
from jax.experimental import pallas as pl
from jax.experimental.pallas import tpu as pltpu
from jax.sharding import PartitionSpec as P

TILE_ROWS = 96
CORES = 2
SIDE = 4
STEPS = (0, 1, 3, 2)
LATE_STEPS = (0, 2, 1, 3)
LOG2_E = 1.4426950408889634
epsilon = 1e-05

f32 = jnp.float32
bf16 = jnp.bfloat16

BOTH_LAST = (((1,), (1,)), ((), ()))

ANY = pl.BlockSpec(memory_space=pl.ANY)
VMEM = pl.BlockSpec(memory_space=pltpu.VMEM)
SMEM = pl.BlockSpec(memory_space=pltpu.SMEM)
PARAMS = pltpu.CompilerParams(vmem_limit_bytes=16 * 1024 * 1024)


def dot(a, b, dims=(((1,), (0,)), ((), ()))):
    return lax.dot_general(a, b, dims, preferred_element_type=f32)


def head_norm(raw_rows, gain_row):
    inverse = lax.rsqrt(jnp.mean(raw_rows * raw_rows, -1, keepdims=True) + epsilon)
    return (raw_rows * inverse * gain_row, inverse)


def head_norm_back(raw_rows, inverse, gain_row, upstream):
    scaled = upstream * gain_row
    return inverse * scaled - raw_rows * (
        inverse * inverse * inverse * jnp.mean(raw_rows * scaled, -1, keepdims=True)
    )


def wrap(i):
    return lax.rem(i + SIDE, SIDE)


def by_core(core, zero, one):
    return jnp.where(core == 0, zero, one)


def copy_kernel(rows_ref, out_ref):
    out_ref[...] = rows_ref[...]


def gather_z_kernel(z_ref, *refs):
    *blocks, out_ref = refs
    for k, block in zip(STEPS, blocks):
        out_ref[wrap(z_ref[0] - k)] = block[...]


def gather_y_kernel(y_ref, *refs):
    *blocks, out_ref = refs
    for k, block in zip(STEPS, blocks):
        y = wrap(y_ref[0] - k)
        for z in range(SIDE):
            out_ref[y * SIDE + z] = block[z]


def project_kernel(core_ref, rows_ref, key_ref, value_ref, *refs):
    *before, out_ref = refs
    kv_heads, _, head = out_ref.shape
    rows = rows_ref[...]
    for kind, weight_ref in enumerate((key_ref, value_ref)):

        @pl.when(core_ref[0] == kind)
        def _(weight_ref=weight_ref):
            for low in range(0, kv_heads, 2):
                pair = dot(rows, weight_ref[:, low * head : (low + 2) * head])
                for i in range(2):
                    here = pair[:, i * head : (i + 1) * head]
                    if before:
                        here = here + before[0][low + i]
                    out_ref[low + i] = here.astype(out_ref.dtype)


def norm_kernel(core_ref, parts_ref, gain_ref, kv_ref, raw_ref):
    total = parts_ref[0].astype(f32)
    for i in range(1, parts_ref.shape[0]):
        total = total + parts_ref[i].astype(f32)
    keys, _ = head_norm(total, gain_ref[...])
    raw_ref[...] = total
    kv_ref[...] = by_core(core_ref[0], keys, total).astype(bf16)


def query_kernel(query_ref, gain_ref, normed_ref):
    head = gain_ref.shape[1]
    for low in range(0, query_ref.shape[1], head):
        cols = slice(low, low + head)
        normed, _ = head_norm(query_ref[:, cols].astype(f32), gain_ref[...])
        normed_ref[:, cols] = normed.astype(bf16)


def attention_kernel(
    core_ref, mine_ref, other_ref, normed_ref, up_ref, seen_ref,
    probs_ref, score_grad_ref, send_ref, keep_ref,
):
    core = core_ref[0]
    rows, head = mine_ref.shape
    text, width = normed_ref.shape
    scale = head ** (-0.5)
    keys = by_core(core, mine_ref[...], other_ref[...])
    values = by_core(core, other_ref[...], mine_ref[...])
    seen = seen_ref[...]
    empty = jnp.where(seen == 0, 1.0, 0.0)
    shown = [jnp.where(i < seen, 1.0, 0.0) for i in range(rows // TILE_ROWS)]
    key_grad = jnp.zeros((rows, head), f32)
    value_grad = jnp.zeros((rows, head), f32)
    for h in range(width // head):
        cols = slice(h * head, (h + 1) * head)
        up = up_ref[:, cols]
        normed = normed_ref[:, cols]
        scores = dot(keys, normed, BOTH_LAST)
        expo = jnp.exp2(scores * (scale * LOG2_E))
        expo = jnp.concatenate(
            [expo[i * TILE_ROWS : (i + 1) * TILE_ROWS] * row for i, row in enumerate(shown)], 0
        )
        totals = jnp.sum(expo, 0, keepdims=True) + empty
        probs = expo * (1.0 / totals)
        probs_low = probs.astype(bf16)
        prob_grad = dot(values, up, BOTH_LAST)
        row_dot = jnp.sum(probs * prob_grad, 0, keepdims=True)
        score_grad = (probs * (prob_grad - row_dot)).astype(bf16)
        key_grad = key_grad + dot(score_grad, normed)
        value_grad = value_grad + dot(probs_low, up)
        probs_ref[h] = probs_low
        score_grad_ref[h] = score_grad
    key_grad = key_grad * scale
    keep_ref[...] = by_core(core, key_grad, value_grad)
    send_ref[...] = by_core(core, value_grad, key_grad).astype(bf16)


def send_heads(held, out_ref, sems, width, fill):
    copies = []
    for h in range(held.shape[1] // width):
        cols = slice(h * width, (h + 1) * width)
        held[:, cols] = fill(h, cols).astype(bf16)
        copies.append(pltpu.make_async_copy(held.at[:, cols], out_ref.at[:, cols], sems.at[h]))
        copies[-1].start()
    for copy in copies:
        copy.wait()


def context_kernel(core_ref, mine_ref, other_ref, probs_ref, context_ref, held, sems):
    values = by_core(core_ref[0], other_ref[...], mine_ref[...])
    values_t = values.astype(f32).T.astype(bf16)
    send_heads(
        held, context_ref, sems, values.shape[1], lambda h, _: dot(values_t, probs_ref[h]).T
    )


def query_grad_kernel(
    core_ref, mine_ref, other_ref, query_ref, gain_ref, score_grad_ref, query_grad_ref, held, sems
):
    keys = by_core(core_ref[0], mine_ref[...], other_ref[...])
    keys_t = keys.astype(f32).T.astype(bf16)
    head = keys.shape[1]
    gain = gain_ref[...]

    def fill(h, cols):
        query = query_ref[:, cols].astype(f32)
        _, inverse = head_norm(query, gain)
        normed_grad = dot(keys_t, score_grad_ref[h]).T * head ** (-0.5)
        return head_norm_back(query, inverse, gain, normed_grad)

    send_heads(held, query_grad_ref, sems, head, fill)


def kv_grad_kernel(core_ref, keep_ref, received_ref, raw_ref, gain_ref, out_ref):
    total = keep_ref[...] + received_ref[...].astype(f32)
    gain = gain_ref[...]
    raw = raw_ref[...]
    _, inverse = head_norm(raw, gain)
    key_raw_grad = head_norm_back(raw, inverse, gain, total)
    kv_grad = by_core(core_ref[0], key_raw_grad, total).astype(bf16)
    for i in range(out_ref.shape[0]):
        out_ref[i] = kv_grad


def image_product(grads_ref, weight_ref, now):
    kv_heads, _, head = grads_ref.shape
    total = None
    for low in range(0, kv_heads, 2):
        pair = jnp.concatenate([grads_ref[low], grads_ref[low + 1]], 1)
        term = dot(pair, weight_ref[now, low * head : (low + 2) * head], BOTH_LAST)
        total = term if total is None else total + term
    return total


def image_kernel(core_ref, grads_ref, key_ref, value_ref, out_ref):
    for kind, weight_ref in enumerate((key_ref, value_ref)):

        @pl.when(core_ref[0] == kind)
        def _(weight_ref=weight_ref):
            out_ref[...] = image_product(grads_ref, weight_ref, slice(None)).astype(out_ref.dtype)


def scatter_y_kernel(y_ref, own_ref, received_ref, keep_ref, *send_refs):
    for k, out_ref in zip(LATE_STEPS, (keep_ref, *send_refs)):
        y = wrap(y_ref[0] + k)
        for z in range(SIDE):
            i = y * SIDE + z
            out_ref[z] = (own_ref[i] + received_ref[i].astype(f32)).astype(out_ref.dtype)


def scatter_z_kernel(z_ref, keep_ref, *refs):
    received, outs, total_ref = refs[: SIDE - 1], refs[SIDE - 1 : -1], refs[-1]
    for z in range(SIDE):
        total = keep_ref[z]
        for block in received:
            total = total + block[z].astype(f32)
        total_ref[z] = total
    for k, out_ref in zip(LATE_STEPS, outs):
        out_ref[...] = total_ref[wrap(z_ref[0] + k)].astype(out_ref.dtype)


def sum_kernel(keep_ref, *refs):
    *received, out_ref = refs
    total = keep_ref[...]
    for block in received:
        total = total + block[...].astype(f32)
    out_ref[...] = total


def weight_grad_kernel(core_ref, rows_ref, mine_ref, other_ref, key_ref, value_ref):
    kv_heads, _, head = mine_ref.shape
    core = core_ref[0]
    rows_t = rows_ref[...].astype(f32).T.astype(bf16)
    for low in range(0, kv_heads, 2):
        cols = slice(low * head, (low + 2) * head)
        mine = jnp.concatenate([mine_ref[low], mine_ref[low + 1]], 1)
        other = jnp.concatenate([other_ref[low], other_ref[low + 1]], 1)
        key_ref[:, cols] = dot(rows_t, by_core(core, mine, other)).astype(bf16)
        value_ref[:, cols] = dot(rows_t, by_core(core, other, mine)).astype(bf16)


def call(kernel, outs, *args, scalar=False, cost=None, scratch=(), to_hbm=()):
    many = len(outs) > 1
    shapes = tuple(jax.ShapeDtypeStruct(shape, kind) for shape, kind in outs)
    places = tuple(ANY if i in to_hbm else VMEM for i in range(len(outs)))
    takes = [VMEM] * len(args)
    if scalar:
        takes[0] = SMEM
    return pl.pallas_call(
        kernel,
        out_shape=shapes if many else shapes[0],
        in_specs=takes,
        out_specs=places if many else places[0],
        scratch_shapes=list(scratch),
        compiler_params=PARAMS,
        cost_estimate=cost,
    )(*args)


def fence(*arrays):
    return lax.optimization_barrier(arrays)


def shards(
    image_rows, queries, key_weight, value_weight, query_gain, key_gain, tiles_seen, context_grad
):
    sections = lax.axis_size("section")
    tp = lax.axis_size("tp")
    chips = tp // CORES
    core = (lax.axis_index("tp") % CORES).astype(jnp.int32).reshape(1)
    same_core = [[i for i in range(tp) if i % CORES == c] for c in range(CORES)]
    swap = [(i, i ^ 1) for i in range(tp)]

    def other_core(x):
        return lax.ppermute(x, "tp", swap)

    def over_chips(x):
        return lax.all_to_all(x, "tp", 0, 0, axis_index_groups=same_core)

    own_rows, features = image_rows.shape
    rows_total = sections * own_rows
    kv_width = key_weight.shape[2]
    head = query_gain.shape[1]
    kv_heads = kv_width // head
    text, width = queries.shape[1:]
    pieces = (kv_heads, rows_total, head)
    square = (rows_total, head)

    key_other = other_core(key_weight[0])
    value_other = other_core(value_weight[0])
    block = (own_rows, features)
    column = (SIDE, *block)
    section = lax.axis_index("section").astype(jnp.int32)
    my_y, my_z = (section // SIDE).reshape(1), (section % SIDE).reshape(1)

    def along_z(x, k):
        to = [(i, i // SIDE * SIDE + (i + k) % SIDE) for i in range(sections)]
        return lax.ppermute(x, "section", to)

    def along_y(x, k):
        return lax.ppermute(x, "section", [(i, (i + k * SIDE) % sections) for i in range(sections)])

    image_rows, core, my_y, my_z = fence(image_rows, core, my_y, my_z)
    others = [along_z(image_rows, k) for k in STEPS[1:]]
    own = call(
        copy_kernel, [(block, bf16)], image_rows,
        cost=pl.CostEstimate(flops=2**30, bytes_accessed=2**20, transcendentals=0),
    )
    rows_z = call(
        gather_z_kernel, [(column, bf16)], my_z, own, *others, scalar=True,
        cost=pl.CostEstimate(flops=2**34, bytes_accessed=2**25, transcendentals=0),
    )
    others = [along_y(rows_z, k) for k in STEPS[1:]]
    blocks = call(
        gather_y_kernel, [((sections, *block), bf16)], my_y, rows_z, *others, scalar=True
    )
    blocks, key_weight, value_weight, key_other, value_other, queries, context_grad = fence(
        blocks, key_weight[0], value_weight[0], key_other, value_other, queries[0], context_grad[0]
    )
    rows = blocks.reshape(rows_total, features)
    rows_other = other_core(rows)
    partial = call(
        project_kernel, [(pieces, f32)], core, rows, key_weight, value_weight, scalar=True
    )
    partial = call(
        project_kernel, [(pieces, bf16)],
        core, rows_other, key_other, value_other, partial, scalar=True,
    )
    parts = over_chips(partial)
    kv_mine, raw = call(
        norm_kernel, [(square, bf16), (square, f32)], core, parts, key_gain, scalar=True
    )
    kv_mine, raw, queries, context_grad = fence(kv_mine, raw, queries, context_grad)
    kv_other = other_core(kv_mine)
    normed = call(
        query_kernel, [((text, width), bf16)], queries, query_gain,
        cost=pl.CostEstimate(flops=2**30, bytes_accessed=2**20, transcendentals=0),
    )
    per_head = (width // head, rows_total, text)
    probs, score_grad, send, keep = call(
        attention_kernel, [(per_head, bf16), (per_head, bf16), (square, bf16), (square, f32)],
        core, kv_mine, kv_other, normed, context_grad, tiles_seen[None], scalar=True,
    )
    send, keep, raw, probs, score_grad = fence(send, keep, raw, probs, score_grad)
    received = other_core(send)
    out_scratch = [
        pltpu.VMEM((text, width), bf16), pltpu.SemaphoreType.DMA((width // head,))
    ]
    copies = call(
        kv_grad_kernel, [(pieces, bf16)], core, keep, received, raw, key_gain, scalar=True
    )
    grads = over_chips(copies)
    image_send = call(
        image_kernel, [((rows_total, features), bf16)],
        core, grads, key_other, value_other, scalar=True,
    )
    image_send, grads, score_grad = fence(image_send, grads, score_grad)
    received = other_core(image_send)
    image_own = call(
        image_kernel, [((rows_total, features), f32)],
        core, grads, key_weight, value_weight, scalar=True,
    )
    image_own, received = fence(image_own, received)
    keep, *sends = call(
        scatter_y_kernel, [(column, f32)] + [(column, bf16)] * (SIDE - 1),
        my_y, image_own.reshape(sections, *block), received.reshape(sections, *block),
        scalar=True,
    )
    keep, sends, rows, grads, probs, score_grad = fence(
        keep, sends, rows, grads, probs, score_grad
    )
    received = [along_y(x, k) for k, x in zip(LATE_STEPS[1:], sends)]
    grads_other = other_core(grads)
    key_weight_grad, value_weight_grad = call(
        weight_grad_kernel, [((features, kv_width), bf16)] * 2,
        core, rows, grads, grads_other, scalar=True,
        cost=pl.CostEstimate(
            flops=2 * features * 2 * kv_width * rows_total,
            bytes_accessed=4 * features * 2 * kv_width,
            transcendentals=0,
        ),
    )
    context = call(
        context_kernel, [((text, width), bf16)], core, kv_mine, kv_other, probs,
        scalar=True, to_hbm=(0,), scratch=out_scratch,
        cost=pl.CostEstimate(flops=2**30, bytes_accessed=2**20, transcendentals=0),
    )
    received, key_weight_grad, value_weight_grad, context, score_grad = fence(
        received, key_weight_grad, value_weight_grad, context, score_grad
    )
    keep, *sends = call(
        scatter_z_kernel, [(block, f32)] + [(block, bf16)] * (SIDE - 1),
        my_z, keep, *received, scalar=True, scratch=[pltpu.VMEM(column, f32)],
    )
    keep, sends, score_grad = fence(keep, sends, score_grad)
    received = [along_z(x, k) for k, x in zip(LATE_STEPS[1:], sends)]
    query_grad = call(
        query_grad_kernel, [((text, width), bf16)],
        core, kv_mine, kv_other, queries, query_gain, score_grad,
        scalar=True, to_hbm=(0,), scratch=out_scratch,
        cost=pl.CostEstimate(flops=2**30, bytes_accessed=2**20, transcendentals=0),
    )
    received, query_grad = fence(received, query_grad)
    image_grad = call(sum_kernel, [(block, f32)], keep, *received)
    return (
        context[None], query_grad[None], key_weight_grad[None], value_weight_grad[None], image_grad
    )


def solution(mesh):
    return jax.shard_map(
        shards,
        mesh=mesh,
        in_specs=(
            P("section", "tp"),
            P("section", None, "tp"),
            P("section", "tp", None),
            P("section", "tp", None),
            P("section", None),
            P("section", None),
            P(),
            P("section", None, "tp"),
        ),
        out_specs=(
            P("section", None, "tp"),
            P("section", None, "tp"),
            P("section", "tp", None),
            P("section", "tp", None),
            P("section", "tp"),
        ),
        check_vma=False,
    )
```

```python
import jax
import jax.numpy as jnp
from jax import lax
from jax.experimental import pallas as pl
from jax.experimental.pallas import tpu as pltpu
from jax.sharding import PartitionSpec as P

TILE_ROWS = 96
CORES = 2
SIDE = 4
STEPS = (0, 1, 3, 2)
LATE_STEPS = (0, 2, 1, 3)
LOG2_E = 1.4426950408889634
epsilon = 1e-05

f32 = jnp.float32
bf16 = jnp.bfloat16

BOTH_LAST = (((1,), (1,)), ((), ()))

ANY = pl.BlockSpec(memory_space=pl.ANY)
VMEM = pl.BlockSpec(memory_space=pltpu.VMEM)
SMEM = pl.BlockSpec(memory_space=pltpu.SMEM)
PARAMS = pltpu.CompilerParams(vmem_limit_bytes=16 * 1024 * 1024)


def dot(a, b, dims=(((1,), (0,)), ((), ()))):
    return lax.dot_general(a, b, dims, preferred_element_type=f32)


def head_norm(raw_rows, gain_row):
    inverse = lax.rsqrt(jnp.mean(raw_rows * raw_rows, -1, keepdims=True) + epsilon)
    return (raw_rows * inverse * gain_row, inverse)


def head_norm_back(raw_rows, inverse, gain_row, upstream):
    scaled = upstream * gain_row
    return inverse * scaled - raw_rows * (
        inverse * inverse * inverse * jnp.mean(raw_rows * scaled, -1, keepdims=True)
    )


def wrap(i):
    return lax.rem(i + SIDE, SIDE)


def by_core(core, zero, one):
    return jnp.where(core == 0, zero, one)


def copy_kernel(rows_ref, out_ref):
    out_ref[...] = rows_ref[...]


def gather_z_kernel(z_ref, *refs):
    *blocks, out_ref = refs
    for k, block in zip(STEPS, blocks):
        out_ref[wrap(z_ref[0] - k)] = block[...]


def gather_y_kernel(y_ref, *refs):
    *blocks, out_ref = refs
    for k, block in zip(STEPS, blocks):
        y = wrap(y_ref[0] - k)
        for z in range(SIDE):
            out_ref[y * SIDE + z] = block[z]


def project_kernel(core_ref, rows_ref, key_ref, value_ref, *refs):
    *before, out_ref = refs
    kv_heads, _, head = out_ref.shape
    rows = rows_ref[...]
    for kind, weight_ref in enumerate((key_ref, value_ref)):

        @pl.when(core_ref[0] == kind)
        def _(weight_ref=weight_ref):
            for low in range(0, kv_heads, 2):
                pair = dot(rows, weight_ref[:, low * head : (low + 2) * head])
                for i in range(2):
                    here = pair[:, i * head : (i + 1) * head]
                    if before:
                        here = here + before[0][low + i]
                    out_ref[low + i] = here.astype(out_ref.dtype)


def norm_kernel(core_ref, parts_ref, gain_ref, kv_ref, raw_ref):
    total = parts_ref[0].astype(f32)
    for i in range(1, parts_ref.shape[0]):
        total = total + parts_ref[i].astype(f32)
    keys, _ = head_norm(total, gain_ref[...])
    raw_ref[...] = total
    kv_ref[...] = by_core(core_ref[0], keys, total).astype(bf16)


def query_kernel(query_ref, gain_ref, normed_ref):
    head = gain_ref.shape[1]
    for low in range(0, query_ref.shape[1], head):
        cols = slice(low, low + head)
        normed, _ = head_norm(query_ref[:, cols].astype(f32), gain_ref[...])
        normed_ref[:, cols] = normed.astype(bf16)


def attention_kernel(
    core_ref, mine_ref, other_ref, normed_ref, up_ref, seen_ref,
    probs_ref, score_grad_ref, send_ref, keep_ref,
):
    core = core_ref[0]
    rows, head = mine_ref.shape
    text, width = normed_ref.shape
    scale = head ** (-0.5)
    keys = by_core(core, mine_ref[...], other_ref[...])
    values = by_core(core, other_ref[...], mine_ref[...])
    seen = seen_ref[...]
    empty = jnp.where(seen == 0, 1.0, 0.0)
    shown = [jnp.where(i < seen, 1.0, 0.0) for i in range(rows // TILE_ROWS)]
    key_grad = jnp.zeros((rows, head), f32)
    value_grad = jnp.zeros((rows, head), f32)
    for h in range(width // head):
        cols = slice(h * head, (h + 1) * head)
        up = up_ref[:, cols]
        normed = normed_ref[:, cols]
        scores = dot(keys, normed, BOTH_LAST)
        expo = jnp.exp2(scores * (scale * LOG2_E))
        expo = jnp.concatenate(
            [expo[i * TILE_ROWS : (i + 1) * TILE_ROWS] * row for i, row in enumerate(shown)], 0
        )
        totals = jnp.sum(expo, 0, keepdims=True) + empty
        probs = expo * (1.0 / totals)
        probs_low = probs.astype(bf16)
        prob_grad = dot(values, up, BOTH_LAST)
        row_dot = jnp.sum(probs * prob_grad, 0, keepdims=True)
        score_grad = (probs * (prob_grad - row_dot)).astype(bf16)
        key_grad = key_grad + dot(score_grad, normed)
        value_grad = value_grad + dot(probs_low, up)
        probs_ref[h] = probs_low
        score_grad_ref[h] = score_grad
    key_grad = key_grad * scale
    keep_ref[...] = by_core(core, key_grad, value_grad)
    send_ref[...] = by_core(core, value_grad, key_grad).astype(bf16)


def send_heads(held, out_ref, sems, width, fill):
    copies = []
    for h in range(held.shape[1] // width):
        cols = slice(h * width, (h + 1) * width)
        held[:, cols] = fill(h, cols).astype(bf16)
        copies.append(pltpu.make_async_copy(held.at[:, cols], out_ref.at[:, cols], sems.at[h]))
        copies[-1].start()
    for copy in copies:
        copy.wait()


def context_kernel(core_ref, mine_ref, other_ref, probs_ref, context_ref, held, sems):
    values = by_core(core_ref[0], other_ref[...], mine_ref[...])
    values_t = values.astype(f32).T.astype(bf16)
    send_heads(
        held, context_ref, sems, values.shape[1], lambda h, _: dot(values_t, probs_ref[h]).T
    )


def query_grad_kernel(
    core_ref, mine_ref, other_ref, query_ref, gain_ref, score_grad_ref, query_grad_ref, held, sems
):
    keys = by_core(core_ref[0], mine_ref[...], other_ref[...])
    keys_t = keys.astype(f32).T.astype(bf16)
    head = keys.shape[1]
    gain = gain_ref[...]

    def fill(h, cols):
        query = query_ref[:, cols].astype(f32)
        _, inverse = head_norm(query, gain)
        normed_grad = dot(keys_t, score_grad_ref[h]).T * head ** (-0.5)
        return head_norm_back(query, inverse, gain, normed_grad)

    send_heads(held, query_grad_ref, sems, head, fill)


def kv_grad_kernel(core_ref, keep_ref, received_ref, raw_ref, gain_ref, out_ref):
    total = keep_ref[...] + received_ref[...].astype(f32)
    gain = gain_ref[...]
    raw = raw_ref[...]
    _, inverse = head_norm(raw, gain)
    key_raw_grad = head_norm_back(raw, inverse, gain, total)
    kv_grad = by_core(core_ref[0], key_raw_grad, total).astype(bf16)
    for i in range(out_ref.shape[0]):
        out_ref[i] = kv_grad


def image_product(grads_ref, weight_ref, now):
    kv_heads, _, head = grads_ref.shape
    total = None
    for low in range(0, kv_heads, 2):
        pair = jnp.concatenate([grads_ref[low], grads_ref[low + 1]], 1)
        term = dot(pair, weight_ref[now, low * head : (low + 2) * head], BOTH_LAST)
        total = term if total is None else total + term
    return total


def image_kernel(core_ref, grads_ref, key_ref, value_ref, out_ref):
    for kind, weight_ref in enumerate((key_ref, value_ref)):

        @pl.when(core_ref[0] == kind)
        def _(weight_ref=weight_ref):
            out_ref[...] = image_product(grads_ref, weight_ref, slice(None)).astype(out_ref.dtype)


def scatter_y_kernel(y_ref, own_ref, received_ref, keep_ref, *send_refs):
    for k, out_ref in zip(LATE_STEPS, (keep_ref, *send_refs)):
        y = wrap(y_ref[0] + k)
        for z in range(SIDE):
            i = y * SIDE + z
            out_ref[z] = (own_ref[i] + received_ref[i].astype(f32)).astype(out_ref.dtype)


def scatter_z_kernel(z_ref, keep_ref, *refs):
    received, outs, total_ref = refs[: SIDE - 1], refs[SIDE - 1 : -1], refs[-1]
    for z in range(SIDE):
        total = keep_ref[z]
        for block in received:
            total = total + block[z].astype(f32)
        total_ref[z] = total
    for k, out_ref in zip(LATE_STEPS, outs):
        out_ref[...] = total_ref[wrap(z_ref[0] + k)].astype(out_ref.dtype)


def sum_kernel(keep_ref, *refs):
    *received, out_ref = refs
    total = keep_ref[...]
    for block in received:
        total = total + block[...].astype(f32)
    out_ref[...] = total


def weight_grad_kernel(core_ref, rows_ref, mine_ref, other_ref, key_ref, value_ref):
    kv_heads, _, head = mine_ref.shape
    core = core_ref[0]
    rows_t = rows_ref[...].astype(f32).T.astype(bf16)
    for low in range(0, kv_heads, 2):
        cols = slice(low * head, (low + 2) * head)
        mine = jnp.concatenate([mine_ref[low], mine_ref[low + 1]], 1)
        other = jnp.concatenate([other_ref[low], other_ref[low + 1]], 1)
        key_ref[:, cols] = dot(rows_t, by_core(core, mine, other)).astype(bf16)
        value_ref[:, cols] = dot(rows_t, by_core(core, other, mine)).astype(bf16)


def call(kernel, outs, *args, scalar=False, cost=None, scratch=(), to_hbm=()):
    many = len(outs) > 1
    shapes = tuple(jax.ShapeDtypeStruct(shape, kind) for shape, kind in outs)
    places = tuple(ANY if i in to_hbm else VMEM for i in range(len(outs)))
    takes = [VMEM] * len(args)
    if scalar:
        takes[0] = SMEM
    return pl.pallas_call(
        kernel,
        out_shape=shapes if many else shapes[0],
        in_specs=takes,
        out_specs=places if many else places[0],
        scratch_shapes=list(scratch),
        compiler_params=PARAMS,
        cost_estimate=cost,
    )(*args)


def fence(*arrays):
    return lax.optimization_barrier(arrays)


def shards(
    image_rows, queries, key_weight, value_weight, query_gain, key_gain, tiles_seen, context_grad
):
    sections = lax.axis_size("section")
    tp = lax.axis_size("tp")
    chips = tp // CORES
    core = (lax.axis_index("tp") % CORES).astype(jnp.int32).reshape(1)
    same_core = [[i for i in range(tp) if i % CORES == c] for c in range(CORES)]
    swap = [(i, i ^ 1) for i in range(tp)]

    def other_core(x):
        return lax.ppermute(x, "tp", swap)

    def over_chips(x):
        return lax.all_to_all(x, "tp", 0, 0, axis_index_groups=same_core)

    own_rows, features = image_rows.shape
    rows_total = sections * own_rows
    kv_width = key_weight.shape[2]
    head = query_gain.shape[1]
    kv_heads = kv_width // head
    text, width = queries.shape[1:]
    pieces = (kv_heads, rows_total, head)
    square = (rows_total, head)

    key_other = other_core(key_weight[0])
    value_other = other_core(value_weight[0])
    block = (own_rows, features)
    column = (SIDE, *block)
    section = lax.axis_index("section").astype(jnp.int32)
    my_y, my_z = (section // SIDE).reshape(1), (section % SIDE).reshape(1)

    def along_z(x, k):
        to = [(i, i // SIDE * SIDE + (i + k) % SIDE) for i in range(sections)]
        return lax.ppermute(x, "section", to)

    def along_y(x, k):
        return lax.ppermute(x, "section", [(i, (i + k * SIDE) % sections) for i in range(sections)])

    image_rows, core, my_y, my_z = fence(image_rows, core, my_y, my_z)
    others = [along_z(image_rows, k) for k in STEPS[1:]]
    own = call(
        copy_kernel, [(block, bf16)], image_rows,
        cost=pl.CostEstimate(flops=2**30, bytes_accessed=2**20, transcendentals=0),
    )
    rows_z = call(
        gather_z_kernel, [(column, bf16)], my_z, own, *others, scalar=True,
        cost=pl.CostEstimate(flops=2**34, bytes_accessed=2**25, transcendentals=0),
    )
    others = [along_y(rows_z, k) for k in STEPS[1:]]
    blocks = call(
        gather_y_kernel, [((sections, *block), bf16)], my_y, rows_z, *others, scalar=True
    )
    blocks, key_weight, value_weight, key_other, value_other, queries, context_grad = fence(
        blocks, key_weight[0], value_weight[0], key_other, value_other, queries[0], context_grad[0]
    )
    rows = blocks.reshape(rows_total, features)
    rows_other = other_core(rows)
    partial = call(
        project_kernel, [(pieces, f32)], core, rows, key_weight, value_weight, scalar=True
    )
    partial = call(
        project_kernel, [(pieces, bf16)],
        core, rows_other, key_other, value_other, partial, scalar=True,
    )
    parts = over_chips(partial)
    kv_mine, raw = call(
        norm_kernel, [(square, bf16), (square, f32)], core, parts, key_gain, scalar=True
    )
    kv_mine, raw, queries, context_grad = fence(kv_mine, raw, queries, context_grad)
    kv_other = other_core(kv_mine)
    normed = call(
        query_kernel, [((text, width), bf16)], queries, query_gain,
        cost=pl.CostEstimate(flops=2**30, bytes_accessed=2**20, transcendentals=0),
    )
    per_head = (width // head, rows_total, text)
    probs, score_grad, send, keep = call(
        attention_kernel, [(per_head, bf16), (per_head, bf16), (square, bf16), (square, f32)],
        core, kv_mine, kv_other, normed, context_grad, tiles_seen[None], scalar=True,
    )
    send, keep, raw, probs, score_grad = fence(send, keep, raw, probs, score_grad)
    received = other_core(send)
    out_scratch = [
        pltpu.VMEM((text, width), bf16), pltpu.SemaphoreType.DMA((width // head,))
    ]
    copies = call(
        kv_grad_kernel, [(pieces, bf16)], core, keep, received, raw, key_gain, scalar=True
    )
    grads = over_chips(copies)
    image_send = call(
        image_kernel, [((rows_total, features), bf16)],
        core, grads, key_other, value_other, scalar=True,
    )
    image_send, grads, score_grad = fence(image_send, grads, score_grad)
    received = other_core(image_send)
    image_own = call(
        image_kernel, [((rows_total, features), f32)],
        core, grads, key_weight, value_weight, scalar=True,
    )
    image_own, received = fence(image_own, received)
    keep, *sends = call(
        scatter_y_kernel, [(column, f32)] + [(column, bf16)] * (SIDE - 1),
        my_y, image_own.reshape(sections, *block), received.reshape(sections, *block),
        scalar=True,
    )
    keep, sends, rows, grads, probs, score_grad = fence(
        keep, sends, rows, grads, probs, score_grad
    )
    received = [along_y(x, k) for k, x in zip(LATE_STEPS[1:], sends)]
    grads_other = other_core(grads)
    key_weight_grad, value_weight_grad = call(
        weight_grad_kernel, [((features, kv_width), bf16)] * 2,
        core, rows, grads, grads_other, scalar=True,
        cost=pl.CostEstimate(
            flops=2 * features * 2 * kv_width * rows_total,
            bytes_accessed=4 * features * 2 * kv_width,
            transcendentals=0,
        ),
    )
    query_grad = call(
        query_grad_kernel, [((text, width), bf16)],
        core, kv_mine, kv_other, queries, query_gain, score_grad,
        scalar=True, to_hbm=(0,), scratch=out_scratch,
        cost=pl.CostEstimate(flops=2**30, bytes_accessed=2**20, transcendentals=0),
    )
    received, key_weight_grad, value_weight_grad, query_grad = fence(
        received, key_weight_grad, value_weight_grad, query_grad
    )
    keep, *sends = call(
        scatter_z_kernel, [(block, f32)] + [(block, bf16)] * (SIDE - 1),
        my_z, keep, *received, scalar=True, scratch=[pltpu.VMEM(column, f32)],
    )
    keep, sends, probs = fence(keep, sends, probs)
    received = [along_z(x, k) for k, x in zip(LATE_STEPS[1:], sends)]
    context = call(
        context_kernel, [((text, width), bf16)], core, kv_mine, kv_other, probs,
        scalar=True, to_hbm=(0,), scratch=out_scratch,
        cost=pl.CostEstimate(flops=2**30, bytes_accessed=2**20, transcendentals=0),
    )
    received, context = fence(received, context)
    image_grad = call(sum_kernel, [(block, f32)], keep, *received)
    return (
        context[None], query_grad[None], key_weight_grad[None], value_weight_grad[None], image_grad
    )


def solution(mesh):
    return jax.shard_map(
        shards,
        mesh=mesh,
        in_specs=(
            P("section", "tp"),
            P("section", None, "tp"),
            P("section", "tp", None),
            P("section", "tp", None),
            P("section", None),
            P("section", None),
            P(),
            P("section", None, "tp"),
        ),
        out_specs=(
            P("section", None, "tp"),
            P("section", None, "tp"),
            P("section", "tp", None),
            P("section", "tp", None),
            P("section", "tp"),
        ),
        check_vma=False,
    )
```

```python
import jax
import jax.numpy as jnp
from jax import lax
from jax.experimental import pallas as pl
from jax.experimental.pallas import tpu as pltpu
from jax.sharding import PartitionSpec as P

TILE_ROWS = 96
CORES = 2
SIDE = 4
STEPS = (0, 1, 3, 2)
LATE_STEPS = (0, 2, 1, 3)
LOG2_E = 1.4426950408889634
epsilon = 1e-05

f32 = jnp.float32
bf16 = jnp.bfloat16

BOTH_LAST = (((1,), (1,)), ((), ()))

ANY = pl.BlockSpec(memory_space=pl.ANY)
VMEM = pl.BlockSpec(memory_space=pltpu.VMEM)
SMEM = pl.BlockSpec(memory_space=pltpu.SMEM)
PARAMS = pltpu.CompilerParams(vmem_limit_bytes=16 * 1024 * 1024)


def dot(a, b, dims=(((1,), (0,)), ((), ()))):
    return lax.dot_general(a, b, dims, preferred_element_type=f32)


def head_norm(raw_rows, gain_row):
    inverse = lax.rsqrt(jnp.mean(raw_rows * raw_rows, -1, keepdims=True) + epsilon)
    return (raw_rows * inverse * gain_row, inverse)


def head_norm_back(raw_rows, inverse, gain_row, upstream):
    scaled = upstream * gain_row
    return inverse * scaled - raw_rows * (
        inverse * inverse * inverse * jnp.mean(raw_rows * scaled, -1, keepdims=True)
    )


def wrap(i):
    return lax.rem(i + SIDE, SIDE)


def by_core(core, zero, one):
    return jnp.where(core == 0, zero, one)


def copy_kernel(rows_ref, out_ref):
    out_ref[...] = rows_ref[...]


def gather_z_kernel(z_ref, *refs):
    *blocks, out_ref = refs
    for k, block in zip(STEPS, blocks):
        out_ref[wrap(z_ref[0] - k)] = block[...]


def gather_y_kernel(y_ref, *refs):
    *blocks, out_ref = refs
    for k, block in zip(STEPS, blocks):
        y = wrap(y_ref[0] - k)
        for z in range(SIDE):
            out_ref[y * SIDE + z] = block[z]


def project_kernel(core_ref, rows_ref, key_ref, value_ref, *refs):
    *before, out_ref = refs
    kv_heads, _, head = out_ref.shape
    rows = rows_ref[...]
    for kind, weight_ref in enumerate((key_ref, value_ref)):

        @pl.when(core_ref[0] == kind)
        def _(weight_ref=weight_ref):
            for low in range(0, kv_heads, 2):
                pair = dot(rows, weight_ref[:, low * head : (low + 2) * head])
                for i in range(2):
                    here = pair[:, i * head : (i + 1) * head]
                    if before:
                        here = here + before[0][low + i]
                    out_ref[low + i] = here.astype(out_ref.dtype)


def norm_kernel(core_ref, parts_ref, gain_ref, kv_ref, raw_ref):
    total = parts_ref[0].astype(f32)
    for i in range(1, parts_ref.shape[0]):
        total = total + parts_ref[i].astype(f32)
    keys, _ = head_norm(total, gain_ref[...])
    raw_ref[...] = total
    kv_ref[...] = by_core(core_ref[0], keys, total).astype(bf16)


def query_kernel(query_ref, gain_ref, normed_ref):
    head = gain_ref.shape[1]
    for low in range(0, query_ref.shape[1], head):
        cols = slice(low, low + head)
        normed, _ = head_norm(query_ref[:, cols].astype(f32), gain_ref[...])
        normed_ref[:, cols] = normed.astype(bf16)


def attention_kernel(
    core_ref, mine_ref, other_ref, normed_ref, up_ref, seen_ref,
    probs_ref, score_grad_ref, send_ref, keep_ref,
):
    core = core_ref[0]
    rows, head = mine_ref.shape
    text, width = normed_ref.shape
    scale = head ** (-0.5)
    keys = by_core(core, mine_ref[...], other_ref[...])
    values = by_core(core, other_ref[...], mine_ref[...])
    seen = seen_ref[...]
    empty = jnp.where(seen == 0, 1.0, 0.0)
    shown = [jnp.where(i < seen, 1.0, 0.0) for i in range(rows // TILE_ROWS)]
    key_grad = jnp.zeros((rows, head), f32)
    value_grad = jnp.zeros((rows, head), f32)
    for h in range(width // head):
        cols = slice(h * head, (h + 1) * head)
        up = up_ref[:, cols]
        normed = normed_ref[:, cols]
        scores = dot(keys, normed, BOTH_LAST)
        expo = jnp.exp2(scores * (scale * LOG2_E))
        expo = jnp.concatenate(
            [expo[i * TILE_ROWS : (i + 1) * TILE_ROWS] * row for i, row in enumerate(shown)], 0
        )
        totals = jnp.sum(expo, 0, keepdims=True) + empty
        probs = expo * (1.0 / totals)
        probs_low = probs.astype(bf16)
        prob_grad = dot(values, up, BOTH_LAST)
        row_dot = jnp.sum(probs * prob_grad, 0, keepdims=True)
        score_grad = (probs * (prob_grad - row_dot)).astype(bf16)
        key_grad = key_grad + dot(score_grad, normed)
        value_grad = value_grad + dot(probs_low, up)
        probs_ref[h] = probs_low
        score_grad_ref[h] = score_grad
    key_grad = key_grad * scale
    keep_ref[...] = by_core(core, key_grad, value_grad)
    send_ref[...] = by_core(core, value_grad, key_grad).astype(bf16)


def send_heads(held, out_ref, sems, width, fill):
    copies = []
    for h in range(held.shape[1] // width):
        cols = slice(h * width, (h + 1) * width)
        held[:, cols] = fill(h, cols).astype(bf16)
        copies.append(pltpu.make_async_copy(held.at[:, cols], out_ref.at[:, cols], sems.at[h]))
        copies[-1].start()
    for copy in copies:
        copy.wait()


def context_kernel(core_ref, mine_ref, other_ref, probs_ref, context_ref, held, sems):
    values = by_core(core_ref[0], other_ref[...], mine_ref[...])
    values_t = values.astype(f32).T.astype(bf16)
    send_heads(
        held, context_ref, sems, values.shape[1], lambda h, _: dot(values_t, probs_ref[h]).T
    )


def query_grad_kernel(
    core_ref, mine_ref, other_ref, query_ref, gain_ref, score_grad_ref, query_grad_ref, held, sems
):
    keys = by_core(core_ref[0], mine_ref[...], other_ref[...])
    keys_t = keys.astype(f32).T.astype(bf16)
    head = keys.shape[1]
    gain = gain_ref[...]

    def fill(h, cols):
        query = query_ref[:, cols].astype(f32)
        _, inverse = head_norm(query, gain)
        normed_grad = dot(keys_t, score_grad_ref[h]).T * head ** (-0.5)
        return head_norm_back(query, inverse, gain, normed_grad)

    send_heads(held, query_grad_ref, sems, head, fill)


def kv_grad_kernel(core_ref, keep_ref, received_ref, raw_ref, gain_ref, out_ref):
    total = keep_ref[...] + received_ref[...].astype(f32)
    gain = gain_ref[...]
    raw = raw_ref[...]
    _, inverse = head_norm(raw, gain)
    key_raw_grad = head_norm_back(raw, inverse, gain, total)
    kv_grad = by_core(core_ref[0], key_raw_grad, total).astype(bf16)
    for i in range(out_ref.shape[0]):
        out_ref[i] = kv_grad


def image_product(grads_ref, weight_ref, now):
    kv_heads, _, head = grads_ref.shape
    total = None
    for low in range(0, kv_heads, 2):
        pair = jnp.concatenate([grads_ref[low], grads_ref[low + 1]], 1)
        term = dot(pair, weight_ref[now, low * head : (low + 2) * head], BOTH_LAST)
        total = term if total is None else total + term
    return total


def image_kernel(core_ref, grads_ref, key_ref, value_ref, out_ref):
    for kind, weight_ref in enumerate((key_ref, value_ref)):

        @pl.when(core_ref[0] == kind)
        def _(weight_ref=weight_ref):
            out_ref[...] = image_product(grads_ref, weight_ref, slice(None)).astype(out_ref.dtype)


def scatter_y_kernel(y_ref, own_ref, received_ref, keep_ref, *send_refs):
    for k, out_ref in zip(LATE_STEPS, (keep_ref, *send_refs)):
        y = wrap(y_ref[0] + k)
        for z in range(SIDE):
            i = y * SIDE + z
            out_ref[z] = (own_ref[i] + received_ref[i].astype(f32)).astype(out_ref.dtype)


def scatter_z_kernel(z_ref, keep_ref, *refs):
    received, outs, total_ref = refs[: SIDE - 1], refs[SIDE - 1 : -1], refs[-1]
    for z in range(SIDE):
        total = keep_ref[z]
        for block in received:
            total = total + block[z].astype(f32)
        total_ref[z] = total
    for k, out_ref in zip(LATE_STEPS, outs):
        out_ref[...] = total_ref[wrap(z_ref[0] + k)].astype(out_ref.dtype)


def sum_kernel(keep_ref, *refs):
    *received, out_ref = refs
    total = keep_ref[...]
    for block in received:
        total = total + block[...].astype(f32)
    out_ref[...] = total


def weight_grad_kernel(core_ref, rows_ref, mine_ref, other_ref, key_ref, value_ref):
    kv_heads, _, head = mine_ref.shape
    core = core_ref[0]
    rows_t = rows_ref[...].astype(f32).T.astype(bf16)
    for low in range(0, kv_heads, 2):
        cols = slice(low * head, (low + 2) * head)
        mine = jnp.concatenate([mine_ref[low], mine_ref[low + 1]], 1)
        other = jnp.concatenate([other_ref[low], other_ref[low + 1]], 1)
        key_ref[:, cols] = dot(rows_t, by_core(core, mine, other)).astype(bf16)
        value_ref[:, cols] = dot(rows_t, by_core(core, other, mine)).astype(bf16)


def call(kernel, outs, *args, scalar=False, cost=None, scratch=(), to_hbm=()):
    many = len(outs) > 1
    shapes = tuple(jax.ShapeDtypeStruct(shape, kind) for shape, kind in outs)
    places = tuple(ANY if i in to_hbm else VMEM for i in range(len(outs)))
    takes = [VMEM] * len(args)
    if scalar:
        takes[0] = SMEM
    return pl.pallas_call(
        kernel,
        out_shape=shapes if many else shapes[0],
        in_specs=takes,
        out_specs=places if many else places[0],
        scratch_shapes=list(scratch),
        compiler_params=PARAMS,
        cost_estimate=cost,
    )(*args)


def fence(*arrays):
    return lax.optimization_barrier(arrays)


def shards(
    image_rows, queries, key_weight, value_weight, query_gain, key_gain, tiles_seen, context_grad
):
    sections = lax.axis_size("section")
    tp = lax.axis_size("tp")
    chips = tp // CORES
    core = (lax.axis_index("tp") % CORES).astype(jnp.int32).reshape(1)
    same_core = [[i for i in range(tp) if i % CORES == c] for c in range(CORES)]
    swap = [(i, i ^ 1) for i in range(tp)]

    def other_core(x):
        return lax.ppermute(x, "tp", swap)

    def over_chips(x):
        return lax.all_to_all(x, "tp", 0, 0, axis_index_groups=same_core)

    own_rows, features = image_rows.shape
    rows_total = sections * own_rows
    kv_width = key_weight.shape[2]
    head = query_gain.shape[1]
    kv_heads = kv_width // head
    text, width = queries.shape[1:]
    pieces = (kv_heads, rows_total, head)
    square = (rows_total, head)

    block = (own_rows, features)
    column = (SIDE, *block)
    section = lax.axis_index("section").astype(jnp.int32)
    my_y, my_z = (section // SIDE).reshape(1), (section % SIDE).reshape(1)

    def along_z(x, k):
        to = [(i, i // SIDE * SIDE + (i + k) % SIDE) for i in range(sections)]
        return lax.ppermute(x, "section", to)

    def along_y(x, k):
        return lax.ppermute(x, "section", [(i, (i + k * SIDE) % sections) for i in range(sections)])

    image_rows, core, my_y, my_z = fence(image_rows, core, my_y, my_z)
    others = [along_z(image_rows, k) for k in STEPS[1:]]
    own = call(
        copy_kernel, [(block, bf16)], image_rows,
        cost=pl.CostEstimate(flops=2**30, bytes_accessed=2**20, transcendentals=0),
    )
    rows_z = call(
        gather_z_kernel, [(column, bf16)], my_z, own, *others, scalar=True,
        cost=pl.CostEstimate(flops=2**34, bytes_accessed=2**25, transcendentals=0),
    )
    rows_z, key_weight, value_weight = fence(rows_z, key_weight, value_weight)
    others = [along_y(rows_z, k) for k in STEPS[1:]]
    key_other = other_core(key_weight[0])
    value_other = other_core(value_weight[0])
    blocks = call(
        gather_y_kernel, [((sections, *block), bf16)], my_y, rows_z, *others, scalar=True
    )
    blocks, key_weight, value_weight, key_other, value_other, queries, context_grad = fence(
        blocks, key_weight[0], value_weight[0], key_other, value_other, queries[0], context_grad[0]
    )
    rows = blocks.reshape(rows_total, features)
    rows_other = other_core(rows)
    partial = call(
        project_kernel, [(pieces, f32)], core, rows, key_weight, value_weight, scalar=True
    )
    partial = call(
        project_kernel, [(pieces, bf16)],
        core, rows_other, key_other, value_other, partial, scalar=True,
    )
    parts = over_chips(partial)
    kv_mine, raw = call(
        norm_kernel, [(square, bf16), (square, f32)], core, parts, key_gain, scalar=True
    )
    kv_mine, raw, queries, context_grad = fence(kv_mine, raw, queries, context_grad)
    kv_other = other_core(kv_mine)
    normed = call(
        query_kernel, [((text, width), bf16)], queries, query_gain,
        cost=pl.CostEstimate(flops=2**30, bytes_accessed=2**20, transcendentals=0),
    )
    per_head = (width // head, rows_total, text)
    probs, score_grad, send, keep = call(
        attention_kernel, [(per_head, bf16), (per_head, bf16), (square, bf16), (square, f32)],
        core, kv_mine, kv_other, normed, context_grad, tiles_seen[None], scalar=True,
    )
    send, keep, raw, probs, score_grad = fence(send, keep, raw, probs, score_grad)
    received = other_core(send)
    out_scratch = [
        pltpu.VMEM((text, width), bf16), pltpu.SemaphoreType.DMA((width // head,))
    ]
    copies = call(
        kv_grad_kernel, [(pieces, bf16)], core, keep, received, raw, key_gain, scalar=True
    )
    grads = over_chips(copies)
    image_send = call(
        image_kernel, [((rows_total, features), bf16)],
        core, grads, key_other, value_other, scalar=True,
    )
    image_send, grads, score_grad = fence(image_send, grads, score_grad)
    received = other_core(image_send)
    image_own = call(
        image_kernel, [((rows_total, features), f32)],
        core, grads, key_weight, value_weight, scalar=True,
    )
    image_own, received = fence(image_own, received)
    keep, *sends = call(
        scatter_y_kernel, [(column, f32)] + [(column, bf16)] * (SIDE - 1),
        my_y, image_own.reshape(sections, *block), received.reshape(sections, *block),
        scalar=True,
    )
    keep, sends, rows, grads, probs, score_grad = fence(
        keep, sends, rows, grads, probs, score_grad
    )
    received = [along_y(x, k) for k, x in zip(LATE_STEPS[1:], sends)]
    grads_other = other_core(grads)
    key_weight_grad, value_weight_grad = call(
        weight_grad_kernel, [((features, kv_width), bf16)] * 2,
        core, rows, grads, grads_other, scalar=True,
        cost=pl.CostEstimate(
            flops=2 * features * 2 * kv_width * rows_total,
            bytes_accessed=4 * features * 2 * kv_width,
            transcendentals=0,
        ),
    )
    query_grad = call(
        query_grad_kernel, [((text, width), bf16)],
        core, kv_mine, kv_other, queries, query_gain, score_grad,
        scalar=True, to_hbm=(0,), scratch=out_scratch,
        cost=pl.CostEstimate(flops=2**30, bytes_accessed=2**20, transcendentals=0),
    )
    received, key_weight_grad, value_weight_grad, query_grad = fence(
        received, key_weight_grad, value_weight_grad, query_grad
    )
    keep, *sends = call(
        scatter_z_kernel, [(block, f32)] + [(block, bf16)] * (SIDE - 1),
        my_z, keep, *received, scalar=True, scratch=[pltpu.VMEM(column, f32)],
    )
    keep, sends, probs = fence(keep, sends, probs)
    received = [along_z(x, k) for k, x in zip(LATE_STEPS[1:], sends)]
    context = call(
        context_kernel, [((text, width), bf16)], core, kv_mine, kv_other, probs,
        scalar=True, to_hbm=(0,), scratch=out_scratch,
        cost=pl.CostEstimate(flops=2**30, bytes_accessed=2**20, transcendentals=0),
    )
    received, context = fence(received, context)
    image_grad = call(sum_kernel, [(block, f32)], keep, *received)
    return (
        context[None], query_grad[None], key_weight_grad[None], value_weight_grad[None], image_grad
    )


def solution(mesh):
    return jax.shard_map(
        shards,
        mesh=mesh,
        in_specs=(
            P("section", "tp"),
            P("section", None, "tp"),
            P("section", "tp", None),
            P("section", "tp", None),
            P("section", None),
            P("section", None),
            P(),
            P("section", None, "tp"),
        ),
        out_specs=(
            P("section", None, "tp"),
            P("section", None, "tp"),
            P("section", "tp", None),
            P("section", "tp", None),
            P("section", "tp"),
        ),
        check_vma=False,
    )
```
